512 devices in a mesh: zone: 16 (over y, core), sub: 32 (over z, x).
Axes of the slice: x: 4, y: 8, z: 8, core: 2. Of those that a mesh axis runs over, the one named last changes fastest.
Arguments:
- diag_blocks: bfloat16 [16, 32, 2, 384, 384], P('zone', 'sub')
- precond_blocks: bfloat16 [16, 32, 2, 384, 384], P('zone', 'sub')
- offdiag_blocks: bfloat16 [16, 32, 2, 4, 384, 384], P('zone', 'sub'), may hold values from -0.09375 to 0.09375
- offdiag_col: int32 [16, 32, 2, 4], P('zone', 'sub'), may hold values from 1 to 10, as said below
- slot_live: int32 [16, 32, 2, 4], P('zone', 'sub'), may hold values from 0 to 1, as said below
- adjoint_rhs: bfloat16 [16, 32, 2, 384, 256], P('zone', 'sub'), may hold values from -6 to 6
- perf_cell: int32 [16, 32, 128], P('zone', 'sub'), may hold values from 0 to 255
- perf_well: int32 [16, 32, 128], P('zone', 'sub'), may hold values from 0 to 2047
- perf_coeff: float32 [16, 32, 3, 128], P('zone', 'sub'), may hold values from -4 to 4
Outputs:
- adjoint: float32 [16, 32, 2, 384, 256], P('zone', 'sub')
- well_gradient: float32 [2048, 256], P(('zone', 'sub'))
The draws below stay inside these ranges and needn't reach their ends.
Inputs may be any that keep to these rules, and one draw needn't show every extreme that they name: `offdiag_col`: entry k of super-block b of a device is a position e of a grid of 3 rows and 4 columns around the device (row e // 4, column e % 4; the device's own super-block b at row 1, column b + 1). The 4 entries of super-block b name, in some order, its four neighbours: rows 0 and 2 at column b + 1, and row 1 at columns b and b + 2. `slot_live`: 1 wherever the neighbour named lies on another device.
All inputs are finite; a program needn't handle non-finite values.
Results may differ from the reference program's by a relative error of at most 0.0026.
Values may be sent and summed in bfloat16 or wider, within the bound.
A program may use at most 64 MiB of HBM per device.

```python
import jax
import jax.numpy as jnp
from jax import lax

CB = 128
BLOCK = 384
B_DEV = 2
OFF = 4
R = 256
ITERS = 3
P_DEV = 128
WELLS = 2048
N_ZONE = 16
N_SUB = 32


def block_noise(key, full_shape):
    return jnp.clip(jax.random.normal(key, full_shape, jnp.float32), -4.0, 4.0)


def dominant_blocks(key, centre, spread):
    full_shape = (N_ZONE, N_SUB, B_DEV, BLOCK, BLOCK)
    eye_mask = (jnp.arange(BLOCK)[:, None] == jnp.arange(BLOCK)[None, :]).astype(jnp.float32)
    noise = block_noise(key, full_shape)
    return (centre * (eye_mask + spread * noise / jnp.sqrt(jnp.float32(BLOCK)))).astype(jnp.bfloat16)


def draw_diag_blocks(key, part):
    key = jax.random.fold_in(key, 3)
    centre_key = jax.random.fold_in(key, 7)
    log_centre = jax.random.uniform(centre_key, (N_ZONE, N_SUB, B_DEV, 1, 1), jnp.float32, -0.9162907, 1.6094379)
    centre = jnp.exp(log_centre)
    return dominant_blocks(jax.random.fold_in(key, 9), centre, 0.3)


def draw_precond_blocks(key, part):
    return dominant_blocks(jax.random.fold_in(key, 5), 0.5, 0.3)


def neighbour_plan(key):
    base_key = jax.random.fold_in(key, 11)
    row_total = N_ZONE * N_SUB * B_DEV
    row_keys = jax.random.split(base_key, row_total)
    neighbour_order = jax.vmap(lambda one_key: jax.random.permutation(one_key, 4))(row_keys)
    row_place = jnp.arange(row_total, dtype=jnp.int32) % B_DEV
    grid_width = B_DEV + 2
    positions = jnp.stack([1 + row_place, 2 * grid_width + 1 + row_place, grid_width + row_place, grid_width + 2 + row_place], axis=1)
    col_ids = jnp.take_along_axis(positions, neighbour_order, axis=1)
    interior = (neighbour_order == 2) & (row_place[:, None] > 0) | (neighbour_order == 3) & (row_place[:, None] < B_DEV - 1)
    coins = jax.random.randint(jax.random.fold_in(base_key, 1), (row_total, 4), 0, 2)
    live_ids = jnp.where(interior, coins, 1)
    return (col_ids.reshape(N_ZONE, N_SUB, B_DEV, 4).astype(jnp.int32), live_ids.reshape(N_ZONE, N_SUB, B_DEV, 4).astype(jnp.int32))


def draw_offdiag_col(key, part):
    return neighbour_plan(key)[0]


def draw_slot_live(key, part):
    return neighbour_plan(key)[1]


def set_ends(drawn, own_key, low, largest):
    longest = drawn.shape.index(max(drawn.shape))
    spots = []
    for shift in (0, 1):
        where = [jax.random.randint(jax.random.fold_in(own_key, axis), (), 0, length) for axis, length in enumerate(drawn.shape)]
        where[longest] = (where[longest] + shift) % drawn.shape[longest]
        spots.append(tuple(where))
    return drawn.at[spots[0]].set(low).at[spots[1]].set(largest)


def levels(own_key, extent, cuts, least, largest):
    def one(dim, blocks):
        steps = jax.random.uniform(jax.random.fold_in(jax.random.fold_in(own_key, 6), dim), (blocks,), jnp.float32, least / len(cuts), largest / len(cuts))
        return jnp.repeat(jnp.exp(steps), extent[dim] // blocks).reshape((-1,) + (1,) * (len(extent) - dim - 1))

    gain = one(*cuts[0])
    for cut in cuts[1:]:
        gain = gain * one(*cut)
    return gain


def centred(rng, dims, width, bound, pieces=(), kind=jnp.bfloat16):
    gain = levels(rng, dims, pieces, -0.22, 0.18) if pieces else 1.0
    drawn = jax.random.normal(rng, dims, jnp.float32) * width * gain
    return jnp.minimum(jnp.maximum(drawn, -bound), bound).astype(kind)


def setup_inputs(seed: int = 0) -> dict:
    keys = jax.random.split(jax.random.key(seed), 10)
    return {
        "diag_blocks": draw_diag_blocks(jax.random.fold_in(keys[9], 71), 0),
        "precond_blocks": draw_precond_blocks(jax.random.fold_in(keys[9], 71), 0),
        "offdiag_blocks": centred(keys[2], (N_ZONE, N_SUB, B_DEV, OFF, BLOCK, BLOCK), (11 * BLOCK) ** -0.5, 0.09375, ((0, 16), (1, 32))),
        "offdiag_col": draw_offdiag_col(jax.random.fold_in(keys[9], 71), 0),
        "slot_live": draw_slot_live(jax.random.fold_in(keys[9], 71), 0),
        "adjoint_rhs": centred(keys[5], (N_ZONE, N_SUB, B_DEV, BLOCK, R), 1.0, 6.0, ((0, 16), (1, 32))),
        "perf_cell": set_ends(jax.random.randint(keys[6], (N_ZONE, N_SUB, P_DEV), 0, B_DEV * CB), jax.random.fold_in(keys[6], 1), 0, (B_DEV * CB) - 1).astype(jnp.int32),
        "perf_well": set_ends(jax.random.randint(keys[7], (N_ZONE, N_SUB, P_DEV), 0, WELLS), jax.random.fold_in(keys[7], 1), 0, WELLS - 1).astype(jnp.int32),
        "perf_coeff": centred(keys[8], (N_ZONE, N_SUB, 3, P_DEV), 0.3, 4.0, ((0, 16), (1, 32)), jnp.float32),
    }


highest = lax.Precision.HIGHEST

def least_squares(columns, rhs_norm):
    count_cols = len(columns)
    basis = []
    triangle = [[None] * count_cols for unused in range(count_cols)]
    for column in range(count_cols):
        residue = columns[column]
        for earlier in range(column):
            weight = lax.optimization_barrier(jnp.sum(basis[earlier] * columns[column], axis=0))
            triangle[earlier][column] = weight
            residue = residue - weight * basis[earlier]
        length = jnp.sqrt(lax.optimization_barrier(jnp.sum(residue * residue, axis=0)))
        triangle[column][column] = length
        basis.append(residue / length)
    solution = [None] * count_cols
    for column in reversed(range(count_cols)):
        summed = rhs_norm * basis[column][0]
        for later_col in range(column + 1, count_cols):
            summed = summed - triangle[column][later_col] * solution[later_col]
        solution[column] = summed / triangle[column][column]
    return solution

def total_inner(left_vec, right_vec):
    return lax.optimization_barrier(jnp.sum(left_vec * right_vec, axis=(0, 1, 2, 3)))

def reference(diag_blocks, precond_blocks, offdiag_blocks, offdiag_col, slot_live, adjoint_rhs, perf_cell, perf_well, perf_coeff):
    zone_count = N_ZONE
    sub_count = N_SUB
    devices_all = zone_count * sub_count
    grid_width = B_DEV + 2
    flat_diag = diag_blocks.reshape(devices_all, B_DEV, BLOCK, BLOCK)
    flat_pre = precond_blocks.reshape(devices_all, B_DEV, BLOCK, BLOCK)
    flat_off = offdiag_blocks.reshape(devices_all, B_DEV, OFF, BLOCK, BLOCK)
    flat_col = offdiag_col.reshape(devices_all, B_DEV, OFF).astype(jnp.int32)
    flat_live = slot_live.reshape(devices_all, B_DEV, OFF)
    device_ids = jnp.arange(devices_all, dtype=jnp.int32)

    def precondition(vector):
        rounded = vector.astype(jnp.bfloat16).reshape(devices_all, B_DEV, BLOCK, vector.shape[-1])

        def one_device(device_item):
            blocks, own_blocks = device_item
            return jnp.einsum('bij,bjr->bir', blocks.astype(jnp.float32), own_blocks.astype(jnp.float32), precision=highest)
        return lax.map(one_device, (flat_pre, rounded)).reshape(vector.shape)

    def apply_operator(vector):
        rounded = vector.astype(jnp.bfloat16)
        group_width = vector.shape[-1]
        plane = rounded.reshape(zone_count, sub_count * B_DEV, BLOCK, group_width)
        padded = jnp.pad(plane, ((1, 1), (1, 1), (0, 0), (0, 0)))
        own_flat = rounded.reshape(devices_all, B_DEV, BLOCK, group_width)

        def one_device(device_item):
            device_no, diagonal, offdiag, col_ids, live_ids, own_blocks = device_item
            zone_no = device_no // sub_count
            sub_no = device_no % sub_count
            summed = jnp.einsum('bij,bjr->bir', diagonal.astype(jnp.float32), own_blocks.astype(jnp.float32), precision=highest)
            grid_rows = zone_no + col_ids // grid_width
            grid_cols = sub_no * B_DEV + col_ids % grid_width
            picked = padded[grid_rows, grid_cols]
            picked = jnp.where(live_ids[:, :, None, None] > 0, picked, jnp.zeros((), jnp.bfloat16))
            return summed + jnp.einsum('bkij,bkjr->bir', offdiag.astype(jnp.float32), picked.astype(jnp.float32), precision=highest)
        mapped = lax.map(one_device, (device_ids, flat_diag, flat_off, flat_col, flat_live, own_flat))
        return mapped.reshape(vector.shape)

    def solve_group(right_side):
        rhs_norm = jnp.sqrt(total_inner(right_side, right_side))
        krylov = [right_side / rhs_norm]
        searches = []
        columns = []
        for iteration in range(ITERS):
            search = precondition(krylov[-1])
            searches.append(search)
            mapped = apply_operator(search)
            heights = [total_inner(earlier, mapped) for earlier in krylov]
            for position in range(len(krylov)):
                mapped = mapped - heights[position] * krylov[position]
            length = jnp.sqrt(total_inner(mapped, mapped))
            if iteration + 1 < ITERS:
                krylov.append(mapped / length)
            entries = heights + [length] + [jnp.zeros_like(length)] * (ITERS - 1 - iteration)
            columns.append(jnp.stack(entries))
        solution = least_squares(columns, rhs_norm)
        result = solution[0] * searches[0]
        for position in range(1, ITERS):
            result = result + solution[position] * searches[position]
        return result
    group_width = min(R, 64)
    groups = R // group_width
    stacked = adjoint_rhs.astype(jnp.float32).reshape(zone_count, sub_count, B_DEV, BLOCK, groups, group_width)
    stacked = jnp.moveaxis(stacked, 4, 0)
    adjoint = lax.map(solve_group, stacked)
    adjoint = jnp.moveaxis(adjoint, 0, 4).reshape(zone_count, sub_count, B_DEV, BLOCK, R)
    lam_rows = adjoint.reshape(devices_all, B_DEV * BLOCK, R)
    cell_ids = perf_cell.reshape(devices_all, P_DEV).astype(jnp.int32)
    phase_ids = jnp.arange(3, dtype=jnp.int32)
    row_index = (cell_ids // CB * BLOCK)[:, None, :] + (phase_ids * CB)[None, :, None] + (cell_ids % CB)[:, None, :]
    picked_rows = jax.vmap(lambda rows_all, index_all: rows_all[index_all])(lam_rows, row_index)
    contrib = -jnp.einsum('dkp,dkpr->dpr', perf_coeff.reshape(devices_all, 3, P_DEV), picked_rows, precision=highest)
    well_gradient = jax.ops.segment_sum(contrib.reshape(devices_all * P_DEV, R), perf_well.reshape(devices_all * P_DEV), num_segments=WELLS)
    return (adjoint, well_gradient)
```

```python
import functools

import jax
import jax.numpy as jnp
from jax import lax
from jax.experimental import pallas as pl
from jax.experimental.pallas import tpu as pltpu
from jax.sharding import PartitionSpec as P

MESH = pl.DeviceIdType.MESH
BF = jnp.bfloat16
F32 = jnp.float32
BLOCK = 384
ROWS = 768
R = 256
ITERS = 3
FAST, SLOW, SIDE = 0, 2, 4
RED_ROWS = (8, 16, 8)


def place():
    zone = lax.axis_index("zone")
    sub = lax.axis_index("sub")
    return zone, sub, zone // 2, lax.rem(zone, 2), sub // 4, lax.rem(sub, 4)


def group(name):
    zone, sub, y, core, z, x = place()
    if name == "xc":
        return 8, core * 4 + x, lambda i: (y * 2 + i // 4, z * 4 + lax.rem(i, 4))
    if name == "y":
        return 8, y, lambda i: (i * 2 + core, sub)
    if name == "z":
        return 8, z, lambda i: (zone, i * 4 + x)
    if name == "zone":
        return 16, zone, lambda i: (i, sub)
    if name == "sub":
        return 32, sub, lambda i: (zone, i)
    pair = sub // 2 * 2
    return 32, zone * 2 + lax.rem(sub, 2), lambda i: (i // 2, pair + lax.rem(i, 2))


def others(name):
    count, me, at = group(name)
    for step in range(1, count):
        slot = lax.rem(me + step, count)
        yield slot, at(slot)


def split(value):
    high = value.astype(BF)
    return high, (value - high.astype(F32)).astype(BF)


def dot(left, right):
    return jnp.dot(left, right, preferred_element_type=F32)


def fold(row):
    return [row[:, :128], row[:, 128:]]


def unfold(tile, position):
    return jnp.concatenate(
        [tile[2 * position : 2 * position + 1], tile[2 * position + 1 : 2 * position + 2]], axis=1
    )


def kernel(
    diag_hbm,
    pre_hbm,
    off_hbm,
    rhs_hbm,
    col_ref,
    live_ref,
    cell_ref,
    well_ref,
    coeff_ref,
    adj_hbm,
    grad_ref,
    diag,
    pre,
    off,
    rhs,
    search,
    image,
    high,
    low,
    near,
    far,
    side,
    red0,
    red1,
    red2,
    pick_high,
    pick_low,
    wells,
    lows,
    contrib,
    spread,
    dense,
    partial,
    piece,
    final,
    turned,
    out,
    load_sem,
    halo_send,
    halo_recv,
    red_send,
    red_recv,
    well_send,
    well_recv,
    store_sem,
):
    zone, sub, y, core, z, x = place()
    reds = (red0, red1, red2)

    loads = [
        pltpu.make_async_copy(src, dst, load_sem.at[i])
        for i, (src, dst) in enumerate(
            ((pre_hbm, pre), (rhs_hbm, rhs), (diag_hbm, diag), (off_hbm, off))
        )
    ]
    for load in loads:
        load.start()

    barrier = pltpu.get_barrier_semaphore()
    greeted = 0
    for name in ("zone", "sub", "pair", "xc"):
        for _, device in others(name):
            pl.semaphore_signal(barrier, inc=1, device_id=device, device_id_type=MESH)
            greeted += 1

    mate = (zone + 1 - 2 * core, sub)
    beyond = (zone - 1 + 2 * core, sub)
    has_far = jnp.logical_and(beyond[0] >= 0, beyond[0] < 16)
    has_side = (sub > 0, sub < 31)
    side_dev = ((zone, sub - 1), (zone, sub + 1))

    @pl.when(jnp.logical_not(has_far))
    def _():
        far[...] = jnp.zeros(far.shape, BF)

    for b in range(2):

        @pl.when(jnp.logical_not(has_side[b]))
        def _():
            side[:, b] = jnp.zeros((ITERS, BLOCK, R), BF)

    def halo(j, b):
        src = high.at[j, pl.ds(b * BLOCK, BLOCK)]
        every = []
        for kind, dst, device, sends, receives in (
            (SIDE, side.at[j, 1 - b], side_dev[b], has_side[b], has_side[1 - b]),
            (SLOW, far.at[j, b], beyond, has_far, has_far),
            (FAST, near.at[j, b], mate, None, None),
        ):
            copy = pltpu.make_async_remote_copy(
                src,
                dst,
                halo_send.at[j, kind + b],
                halo_recv.at[j, kind + b],
                device_id=device,
                device_id_type=MESH,
            )
            every.append((copy, sends, receives))
        return every

    def guarded(condition, action):
        if condition is None:
            action()
        else:
            pl.when(condition)(action)

    def halo_start(j, b):
        for copy, sends, _ in halo(j, b):
            guarded(sends, copy.start)

    def halo_wait(j, which):
        for b in range(2):
            copy, _, receives = halo(j, b)[which]
            guarded(receives, copy.wait_recv)

    def precondition(j, b, value):
        if j == 0:
            found = dot(pre[b], value)
        else:
            upper, lower = split(value)
            found = dot(pre[b], upper) + dot(pre[b], lower)
        rows = pl.ds(b * BLOCK, BLOCK)
        search[j, rows] = found
        upper, lower = split(found)
        high[j, rows] = upper
        low[j, rows] = lower

    def slot_of(b, position):
        where = 0
        for k in range(1, 4):
            where = where + jnp.where(col_ref[b, k] == position, k, 0)
        return b * 4 + where

    def live_of(b, position):
        found = 0
        for k in range(4):
            found = found + jnp.where(col_ref[b, k] == position, live_ref[b, k], 0)
        return found

    def local_products(j):
        for b in range(2):
            mine = pl.ds(b * BLOCK, BLOCK)
            other = pl.ds((1 - b) * BLOCK, BLOCK)
            total = dot(diag[b], high[j, mine]) + dot(diag[b], low[j, mine])
            block = off[slot_of(b, 6 - b)]
            inner = dot(block, high[j, other]) + dot(block, low[j, other])
            image[j, mine] = total + jnp.where(live_of(b, 6 - b) > 0, inner, 0.0)

    def halo_products(j):
        halo_wait(j, 2)
        for b in range(2):
            position = jnp.where(core == 0, 9 + b, 1 + b)
            image[j, pl.ds(b * BLOCK, BLOCK)] += dot(off[slot_of(b, position)], near[j, b])
        halo_wait(j, 0)
        for b in range(2):
            image[j, pl.ds(b * BLOCK, BLOCK)] += dot(off[slot_of(b, 4 + 3 * b)], side[j, b])
        halo_wait(j, 1)
        for b in range(2):
            position = jnp.where(core == 0, 1 + b, 9 + b)
            image[j, pl.ds(b * BLOCK, BLOCK)] += dot(off[slot_of(b, position)], far[j, b])

    stages = ("xc", "y", "z")

    def red_start(which, stage, value):
        buf = reds[which].at[stage]
        _, me, _ = group(stages[stage])
        buf[me] = value
        for _, device in others(stages[stage]):
            pltpu.make_async_remote_copy(
                buf.at[me],
                buf.at[me],
                red_send.at[which, stage],
                red_recv.at[which, stage],
                device_id=device,
                device_id_type=MESH,
            ).start()

    def red_finish(which, stage):
        buf = reds[which].at[stage]
        seven = buf.at[pl.ds(0, 7)]
        pltpu.make_async_copy(seven, seven, red_recv.at[which, stage]).wait()
        total = buf[0]
        for i in range(1, 8):
            total = total + buf[i]
        if which == 0:
            largest = buf[0]
            for i in range(1, 8):
                largest = jnp.maximum(largest, buf[i])
            row = lax.broadcasted_iota(jnp.int32, total.shape, 0)
            total = jnp.where(row < 2, total, largest)
        return total

    def inner_products(makers, pairs):
        step = 64

        def body(i, sums):
            rows = pl.ds(pl.multiple_of(i * step, step), step)
            vectors = [make(rows) for make in makers]
            return tuple(
                total + jnp.sum((vectors[a] * vectors[c]).reshape(step // 8, 8, R), axis=0)
                for total, (a, c) in zip(sums, pairs)
            )

        sums = lax.fori_loop(
            0, ROWS // step, body, tuple(jnp.zeros((8, R), F32) for _ in pairs)
        )
        return [jnp.sum(total, axis=0, keepdims=True) for total in sums]

    def payload(values, rows):
        pieces = [half for value in values for half in fold(value)]
        if len(pieces) < rows:
            pieces.append(jnp.zeros((rows - len(pieces), 128), F32))
        return jnp.concatenate(pieces, axis=0)

    def largest_of(ref, count):
        def body(i, best):
            return jnp.maximum(best, jnp.max(jnp.abs(ref[i].astype(F32).reshape(48, 8, BLOCK)), axis=0))

        best = lax.fori_loop(0, count, body, jnp.zeros((8, BLOCK), F32))
        return jnp.max(jnp.max(best, axis=0, keepdims=True), axis=1, keepdims=True)

    def wells_start():
        wells[zone] = well_ref[...]
        for _, device in others("zone"):
            pltpu.make_async_remote_copy(
                wells.at[zone],
                wells.at[zone],
                well_send.at[3],
                well_recv.at[3],
                device_id=device,
                device_id_type=MESH,
            ).start()

    def pick_build():
        cells = cell_ref[...]
        for b in range(2):
            for q in range(3):
                row = lax.broadcasted_iota(jnp.int32, (128, 128), 0) + b * 128
                value = jnp.where(row == cells, -coeff_ref[q : q + 1, :], 0.0)
                upper, lower = split(value)
                rows = pl.ds(b * BLOCK + q * 128, 128)
                pick_high[rows] = upper
                pick_low[rows] = lower

    def lows_build():
        fifteen = wells.at[pl.ds(0, 15)]
        pltpu.make_async_copy(fifteen, fifteen, well_recv.at[3]).wait()

        def body(i, carry):
            ids = wells[i]
            code = ((ids >> 7) << 3) + (ids & 7)
            row = lax.broadcasted_iota(jnp.int32, (128, 128), 0)
            lows[i] = jnp.where(row == code, 1.0, 0.0).astype(BF)
            return carry

        lax.fori_loop(0, 16, body, 0)

    def turned_dot(left, right):
        return lax.dot_general(left, right, (((0,), (0,)), ((), ())), preferred_element_type=F32)

    def contrib_start(j):
        value = (
            turned_dot(high[j], pick_high[...])
            + turned_dot(low[j], pick_high[...])
            + turned_dot(high[j], pick_low[...])
        )
        contrib[j] = value.reshape(16, 16, 128)
        spread[j, zone] = contrib[j, zone]
        for slot, device in others("zone"):
            pltpu.make_async_remote_copy(
                contrib.at[j, slot],
                spread.at[j, zone],
                well_send.at[j],
                well_recv.at[j],
                device_id=device,
                device_id_type=MESH,
            ).start()

    def dense_start(j):
        fifteen = spread.at[j, pl.ds(0, 15)]
        pltpu.make_async_copy(fifteen, fifteen, well_recv.at[j]).wait()

        def body(i, total):
            chunk = (wells[i] >> 3) & 15
            value = spread[j, i]
            placed = jnp.concatenate([jnp.where(chunk == k, value, 0.0) for k in range(16)], axis=0)
            upper, lower = split(placed)
            return total + lax.dot_general(
                jnp.concatenate([upper, lower], axis=0),
                lows[i],
                (((1,), (1,)), ((), ())),
                preferred_element_type=F32,
            )

        total = lax.fori_loop(0, 16, body, jnp.zeros((512, 128), F32))
        dense[j] = (total[:256] + total[256:]).reshape(32, 8, 128)
        partial[j, sub] = dense[j, sub]
        for slot, device in others("sub"):
            pltpu.make_async_remote_copy(
                dense.at[j, slot],
                partial.at[j, sub],
                well_send.at[4 + j],
                well_recv.at[4 + j],
                device_id=device,
                device_id_type=MESH,
            ).start()

    def dense_finish(j):
        most = partial.at[j, pl.ds(0, 31)]
        pltpu.make_async_copy(most, most, well_recv.at[4 + j]).wait()
        total = partial[j, 0]
        for i in range(1, 32):
            total = total + partial[j, i]
        piece[j] = total

    loads[0].wait()
    loads[1].wait()
    for b in range(2):
        precondition(0, b, rhs[pl.ds(b * BLOCK, BLOCK)])
    right_side = lambda rows: rhs[rows].astype(F32)
    (square,) = inner_products([right_side], [(0, 0)])
    pick_build()
    loads[2].wait()
    loads[3].wait()
    pl.semaphore_wait(barrier, greeted)
    for b in range(2):
        halo_start(0, b)
    wells_start()
    size_pre = largest_of(pre, 2)
    size_op = jnp.maximum(largest_of(diag, 2), largest_of(off, 8))
    red_start(
        0,
        0,
        jnp.concatenate(
            fold(square)
            + [
                jnp.broadcast_to(size_pre, (1, 128)),
                jnp.broadcast_to(size_op, (1, 128)),
                jnp.zeros((4, 128), F32),
            ],
            axis=0,
        ),
    )
    contrib_start(0)
    local_products(0)
    red_start(0, 1, red_finish(0, 0))
    halo_products(0)

    for b in range(2):
        precondition(1, b, image[0, pl.ds(b * BLOCK, BLOCK)])
        halo_start(1, b)
    contrib_start(1)
    local_products(1)
    red_start(0, 2, red_finish(0, 1))
    lows_build()
    dense_start(0)
    halo_products(1)

    sizes = red_finish(0, 2)
    rhs_norm = jnp.sqrt(unfold(sizes, 0))
    inverse = 1.0 / rhs_norm
    shrink = 1.0 / (
        jnp.concatenate([sizes[2:3], sizes[2:3]], axis=1)
        * jnp.concatenate([sizes[3:4], sizes[3:4]], axis=1)
    )
    scale1 = inverse * shrink
    for b in range(2):
        precondition(2, b, image[1, pl.ds(b * BLOCK, BLOCK)] * scale1)
        halo_start(2, b)
    unit = lambda rows: rhs[rows].astype(F32) * inverse
    first = lambda rows: image[0, rows] * inverse
    second = lambda rows: image[1, rows] * scale1
    third = lambda rows: image[2, rows] * shrink
    early = inner_products([unit, first, second], [(0, 1), (0, 2), (1, 1), (1, 2), (2, 2)])
    red_start(1, 0, payload(early, 16))
    contrib_start(2)
    local_products(2)
    red_start(1, 1, red_finish(1, 0))
    dense_start(1)
    halo_products(2)

    late = inner_products([unit, first, second, third], [(0, 3), (1, 3), (2, 3), (3, 3)])
    red_start(2, 0, payload(late, 8))
    dense_start(2)
    red_start(2, 1, red_finish(2, 0))
    red_start(1, 2, red_finish(1, 1))
    dense_finish(0)
    dense_finish(1)
    red_start(2, 2, red_finish(2, 1))
    head = red_finish(1, 2)
    g0, g1, m00, m01, m11 = [unfold(head, i) for i in range(5)]
    dense_finish(2)
    tail = red_finish(2, 2)
    g2, m02, m12, m22 = [unfold(tail, i) for i in range(4)]

    e01 = m01 / m00
    e02 = m02 / m00
    p11 = m11 - e01 * m01
    p12 = m12 - e01 * m02
    e12 = p12 / p11
    p22 = m22 - e02 * m02 - e12 * p12
    f0 = g0
    f1 = g1 - e01 * f0
    f2 = g2 - e02 * f0 - e12 * f1
    c2 = f2 / p22
    c1 = f1 / p11 - e12 * c2
    c0 = f0 / m00 - e01 * c1 - e02 * c2
    coeffs = [c0, c1 * shrink, c2 * shrink * rhs_norm]

    lane = lax.broadcasted_iota(jnp.int32, (8, R), 1)
    row = lax.broadcasted_iota(jnp.int32, (8, R), 0)
    mine = lane == row + (zone * 16 + lax.rem(sub, 2) * 8)
    tile = jnp.zeros((8, 128), F32)
    for j in range(ITERS):
        factor = jnp.sum(jnp.where(mine, coeffs[j], 0.0), axis=1, keepdims=True)
        tile = tile + factor * piece[j]
    _, me, _ = group("pair")
    final[me] = tile
    for _, device in others("pair"):
        pltpu.make_async_remote_copy(
            final.at[me],
            final.at[me],
            well_send.at[7],
            well_recv.at[7],
            device_id=device,
            device_id_type=MESH,
        ).start()

    stores = []
    for b in range(2):
        for half in range(2):
            rows = pl.ds(b * BLOCK + half * 192, 192)
            total = coeffs[0] * search[0, rows]
            for j in range(1, ITERS):
                total = total + coeffs[j] * search[j, rows]
            out[rows] = total
            store = pltpu.make_async_copy(out.at[rows], adj_hbm.at[rows], store_sem.at[b * 2 + half])
            store.start()
            stores.append(store)

    most = final.at[pl.ds(0, 31)]
    pltpu.make_async_copy(most, most, well_recv.at[7]).wait()
    gathered = final[...].reshape(R, 128)
    turned[...] = jnp.concatenate([gathered[:128].T, gathered[128:].T], axis=1)
    eight = turned[pl.ds(pl.multiple_of(zone * 8, 8), 8)]
    grad_ref[...] = jnp.where(lax.rem(sub, 2) == 0, eight[:4], eight[4:])

    for store in stores:
        store.wait()
    for j in range(ITERS):
        for b in range(2):
            for copy, sends, _ in halo(j, b):
                guarded(sends, copy.wait_send)
    for which in range(3):
        for stage in range(3):
            seven = reds[which].at[stage, pl.ds(0, 7)]
            pltpu.make_async_copy(seven, seven, red_send.at[which, stage]).wait()
    for j in range(ITERS):
        fifteen = spread.at[j, pl.ds(0, 15)]
        pltpu.make_async_copy(fifteen, fifteen, well_send.at[j]).wait()
        most = partial.at[j, pl.ds(0, 31)]
        pltpu.make_async_copy(most, most, well_send.at[4 + j]).wait()
    fifteen = wells.at[pl.ds(0, 15)]
    pltpu.make_async_copy(fifteen, fifteen, well_send.at[3]).wait()
    most = final.at[pl.ds(0, 31)]
    pltpu.make_async_copy(most, most, well_send.at[7]).wait()


def shards(
    diag_blocks,
    precond_blocks,
    offdiag_blocks,
    offdiag_col,
    slot_live,
    adjoint_rhs,
    perf_cell,
    perf_well,
    perf_coeff,
):
    any_spec = pl.BlockSpec(memory_space=pl.ANY)
    smem = pl.BlockSpec(memory_space=pltpu.SMEM)
    vmem = pl.BlockSpec(memory_space=pltpu.VMEM)
    dma = pltpu.SemaphoreType.DMA
    adjoint, gradient = pl.pallas_call(
        kernel,
        out_shape=(
            jax.ShapeDtypeStruct((ROWS, R), F32),
            jax.ShapeDtypeStruct((4, R), F32),
        ),
        in_specs=[any_spec] * 4 + [smem] * 2 + [vmem] * 3,
        out_specs=(any_spec, vmem),
        scratch_shapes=[
            pltpu.VMEM((2, BLOCK, BLOCK), BF),
            pltpu.VMEM((2, BLOCK, BLOCK), BF),
            pltpu.VMEM((8, BLOCK, BLOCK), BF),
            pltpu.VMEM((ROWS, R), BF),
            pltpu.VMEM((ITERS, ROWS, R), F32),
            pltpu.VMEM((ITERS, ROWS, R), F32),
            pltpu.VMEM((ITERS, ROWS, R), BF),
            pltpu.VMEM((ITERS, ROWS, R), BF),
            pltpu.VMEM((ITERS, 2, BLOCK, R), BF),
            pltpu.VMEM((ITERS, 2, BLOCK, R), BF),
            pltpu.VMEM((ITERS, 2, BLOCK, R), BF),
            pltpu.VMEM((3, 8, 8, 128), F32),
            pltpu.VMEM((3, 8, 16, 128), F32),
            pltpu.VMEM((3, 8, 8, 128), F32),
            pltpu.VMEM((ROWS, 128), BF),
            pltpu.VMEM((ROWS, 128), BF),
            pltpu.VMEM((16, 1, 128), jnp.int32),
            pltpu.VMEM((16, 128, 128), BF),
            pltpu.VMEM((ITERS, 16, 16, 128), F32),
            pltpu.VMEM((ITERS, 16, 16, 128), F32),
            pltpu.VMEM((ITERS, 32, 8, 128), F32),
            pltpu.VMEM((ITERS, 32, 8, 128), F32),
            pltpu.VMEM((ITERS, 8, 128), F32),
            pltpu.VMEM((32, 8, 128), F32),
            pltpu.VMEM((128, R), F32),
            pltpu.VMEM((ROWS, R), F32),
            dma((4,)),
            dma((ITERS, 6)),
            dma((ITERS, 6)),
            dma((3, 3)),
            dma((3, 3)),
            dma((8,)),
            dma((8,)),
            dma((4,)),
        ],
        compiler_params=pltpu.CompilerParams(
            collective_id=0, has_side_effects=True, vmem_limit_bytes=44 * 1024 * 1024
        ),
        name="adjoint_solve",
    )(
        diag_blocks.reshape(2, BLOCK, BLOCK),
        precond_blocks.reshape(2, BLOCK, BLOCK),
        offdiag_blocks.reshape(8, BLOCK, BLOCK),
        adjoint_rhs.reshape(ROWS, R),
        offdiag_col.reshape(2, 4),
        slot_live.reshape(2, 4),
        perf_cell.reshape(1, 128),
        perf_well.reshape(1, 128),
        perf_coeff.reshape(3, 128),
    )
    return adjoint.reshape(1, 1, 2, BLOCK, R), gradient


def solution(mesh):
    placed = (
        P("zone", "sub", None, None, None),
        P("zone", "sub", None, None, None),
        P("zone", "sub", None, None, None, None),
        P("zone", "sub", None, None),
        P("zone", "sub", None, None),
        P("zone", "sub", None, None, None),
        P("zone", "sub", None),
        P("zone", "sub", None),
        P("zone", "sub", None, None),
    )
    return jax.shard_map(
        shards,
        mesh=mesh,
        in_specs=placed,
        out_specs=(P("zone", "sub", None, None, None), P(("zone", "sub"), None)),
        check_vma=False,
    )
```

```python
import functools

import jax
import jax.numpy as jnp
from jax import lax
from jax.experimental import pallas as pl
from jax.experimental.pallas import tpu as pltpu
from jax.sharding import PartitionSpec as P

MESH = pl.DeviceIdType.MESH
BF = jnp.bfloat16
F32 = jnp.float32
BLOCK = 384
ROWS = 768
R = 256
ITERS = 3
OFF_MOST = 0.09375
FAST, SLOW, SIDE = 0, 2, 4
RED_ROWS = (8, 16, 8)


def place():
    zone = lax.axis_index("zone")
    sub = lax.axis_index("sub")
    return zone, sub, zone // 2, lax.rem(zone, 2), sub // 4, lax.rem(sub, 4)


def group(name):
    zone, sub, y, core, z, x = place()
    if name == "xc":
        return 8, core * 4 + x, lambda i: (y * 2 + i // 4, z * 4 + lax.rem(i, 4))
    if name == "y":
        return 8, y, lambda i: (i * 2 + core, sub)
    if name == "z":
        return 8, z, lambda i: (zone, i * 4 + x)
    if name == "zone":
        return 16, zone, lambda i: (i, sub)
    if name == "sub":
        return 32, sub, lambda i: (zone, i)
    pair = sub // 2 * 2
    return 32, zone * 2 + lax.rem(sub, 2), lambda i: (i // 2, pair + lax.rem(i, 2))


def others(name):
    count, me, at = group(name)
    for step in range(1, count):
        slot = lax.rem(me + step, count)
        yield slot, at(slot)


def split(value):
    high = value.astype(BF)
    return high, (value - high.astype(F32)).astype(BF)


def dot(left, right):
    return jnp.dot(left, right, preferred_element_type=F32)


def kernel(
    diag_hbm,
    pre_hbm,
    off_hbm,
    rhs_hbm,
    col_ref,
    live_ref,
    cell_ref,
    well_ref,
    coeff_ref,
    adj_hbm,
    grad_ref,
    diag,
    pre,
    off,
    rhs,
    search,
    image,
    high,
    low,
    near,
    far,
    side,
    red0,
    red1,
    red2,
    pick,
    wells,
    lows,
    hots,
    contrib,
    spread,
    placed,
    dense,
    partial,
    final,
    turned,
    out,
    load_sem,
    halo_send,
    halo_recv,
    red_send,
    red_recv,
    well_send,
    well_recv,
    store_sem,
):
    zone, sub, y, core, z, x = place()
    reds = (red0, red1, red2)

    loads = [
        pltpu.make_async_copy(src, dst, load_sem.at[i])
        for i, (src, dst) in enumerate(
            ((pre_hbm, pre), (rhs_hbm, rhs), (diag_hbm, diag), (off_hbm, off))
        )
    ]
    for load in loads:
        load.start()

    barrier = pltpu.get_barrier_semaphore()
    greeted = 0
    for name in ("zone", "sub", "pair", "xc"):
        for _, device in others(name):
            pl.semaphore_signal(barrier, inc=1, device_id=device, device_id_type=MESH)
            greeted += 1

    mate = (zone + 1 - 2 * core, sub)
    beyond = (zone - 1 + 2 * core, sub)
    has_far = jnp.logical_and(beyond[0] >= 0, beyond[0] < 16)
    has_side = (sub > 0, sub < 31)
    side_dev = ((zone, sub - 1), (zone, sub + 1))

    @pl.when(jnp.logical_not(has_far))
    def _():
        far[...] = jnp.zeros(far.shape, BF)

    for b in range(2):

        @pl.when(jnp.logical_not(has_side[b]))
        def _():
            side[:, :, b] = jnp.zeros((ITERS, 2, BLOCK, 128), BF)

    def halo(j, h, kind, b):
        src = high.at[j, h, pl.ds(b * BLOCK, BLOCK)]
        dst, device, sends, receives = {
            SIDE: (side.at[j, h, 1 - b], side_dev[b], has_side[b], has_side[1 - b]),
            SLOW: (far.at[j, h, b], beyond, has_far, has_far),
            FAST: (near.at[j, h, b], mate, None, None),
        }[kind]
        copy = pltpu.make_async_remote_copy(
            src,
            dst,
            halo_send.at[j, h, kind + b],
            halo_recv.at[j, h, kind + b],
            device_id=device,
            device_id_type=MESH,
        )
        return copy, sends, receives

    def guarded(condition, action):
        if condition is None:
            action()
        else:
            pl.when(condition)(action)

    def halo_start(j, h):
        for b in range(2):
            for kind in (SLOW, SIDE, FAST):
                copy, sends, _ = halo(j, h, kind, b)
                guarded(sends, copy.start)

    def halo_wait(j, h, kind):
        for b in range(2):
            copy, _, receives = halo(j, h, kind, b)
            guarded(receives, copy.wait_recv)

    def keep(j, h, b, found):
        rows = pl.ds(b * BLOCK, BLOCK)
        search[j, h, rows] = found
        upper, lower = split(found)
        high[j, h, rows] = upper
        low[j, h, rows] = lower

    def both(left, upper, lower):
        found = dot(left, jnp.concatenate([upper, lower], axis=1))
        return found[:, :128] + found[:, 128:]

    def precondition(j, h, scale):
        for b in range(2):
            upper, lower = split(image[j - 1, h, pl.ds(b * BLOCK, BLOCK)])
            found = both(pre[b], upper, lower)
            keep(j, h, b, found if scale is None else found * scale())

    def slot_of(b, position):
        where = 0
        for k in range(1, 4):
            where = where + jnp.where(col_ref[b, k] == position, k, 0)
        return b * 4 + where

    def live_of(b, position):
        found = 0
        for k in range(4):
            found = found + jnp.where(col_ref[b, k] == position, live_ref[b, k], 0)
        return found

    def local_products(j, h):
        for b in range(2):
            mine = pl.ds(b * BLOCK, BLOCK)
            other = pl.ds((1 - b) * BLOCK, BLOCK)
            total = both(diag[b], high[j, h, mine], low[j, h, mine])
            inner = both(off[slot_of(b, 6 - b)], high[j, h, other], low[j, h, other])
            image[j, h, mine] = total + jnp.where(live_of(b, 6 - b) > 0, inner, 0.0)

    def halo_products(j, h):
        def add(b, position, block):
            image[j, h, pl.ds(b * BLOCK, BLOCK)] += dot(off[slot_of(b, position)], block)

        halo_wait(j, h, FAST)
        for b in range(2):
            add(b, jnp.where(core == 0, 9 + b, 1 + b), near[j, h, b])
        halo_wait(j, h, SIDE)
        for b in range(2):
            add(b, 4 + 3 * b, side[j, h, b])
        halo_wait(j, h, SLOW)
        for b in range(2):
            add(b, jnp.where(core == 0, 1 + b, 9 + b), far[j, h, b])

    stages = ("xc", "y", "z")

    def red_start(which, stage, value):
        buf = reds[which].at[stage]
        _, me, _ = group(stages[stage])
        buf[me] = value
        for _, device in others(stages[stage]):
            pltpu.make_async_remote_copy(
                buf.at[me],
                buf.at[me],
                red_send.at[which, stage],
                red_recv.at[which, stage],
                device_id=device,
                device_id_type=MESH,
            ).start()

    def red_finish(which, stage):
        buf = reds[which].at[stage]
        seven = buf.at[pl.ds(0, 7)]
        pltpu.make_async_copy(seven, seven, red_recv.at[which, stage]).wait()
        total = buf[0]
        for i in range(1, 8):
            total = total + buf[i]
        if which == 0:
            largest = buf[0]
            for i in range(1, 8):
                largest = jnp.maximum(largest, buf[i])
            row = lax.broadcasted_iota(jnp.int32, total.shape, 0)
            total = jnp.where(row < 2, total, largest)
        return total

    def inner_products(makers, pairs):
        step = 128

        def body(i, sums):
            rows = pl.ds(pl.multiple_of(i * step, step), step)
            vectors = [make(rows) for make in makers]
            return tuple(
                total + jnp.sum((vectors[a] * vectors[c]).reshape(step // 8, 8, 128), axis=0)
                for total, (a, c) in zip(sums, pairs)
            )

        sums = lax.fori_loop(
            0, ROWS // step, body, tuple(jnp.zeros((8, 128), F32) for _ in pairs)
        )
        return [jnp.sum(total, axis=0, keepdims=True) for total in sums]

    def payload(values, rows):
        pieces = [half for pair in zip(*values) for half in pair]
        if len(pieces) < rows:
            pieces.append(jnp.zeros((rows - len(pieces), 128), F32))
        return jnp.concatenate(pieces, axis=0)

    def largest_of(ref, count):
        def body(i, best):
            return jnp.maximum(best, jnp.max(jnp.abs(ref[i].astype(F32).reshape(48, 8, BLOCK)), axis=0))

        best = lax.fori_loop(0, count, body, jnp.zeros((8, BLOCK), F32))
        return jnp.max(jnp.max(best, axis=0, keepdims=True), axis=1, keepdims=True)

    def wells_start():
        wells[zone] = well_ref[...]
        for _, device in others("zone"):
            pltpu.make_async_remote_copy(
                wells.at[zone],
                wells.at[zone],
                well_send.at[3],
                well_recv.at[3],
                device_id=device,
                device_id_type=MESH,
            ).start()

    def pick_build():
        cells = cell_ref[...]
        for b in range(2):
            for q in range(3):
                row = lax.broadcasted_iota(jnp.int32, (128, 128), 0) + b * 128
                upper, lower = split(jnp.where(row == cells, -coeff_ref[q], 0.0).T)
                columns = pl.ds(b * BLOCK + q * 128, 128)
                pick[pl.ds(0, 128), columns] = upper
                pick[pl.ds(128, 128), columns] = lower

    def lows_build():
        fifteen = wells.at[pl.ds(0, 15)]
        pltpu.make_async_copy(fifteen, fifteen, well_recv.at[3]).wait()

        def body(i, carry):
            ids = wells[i]
            code = ((ids >> 7) << 3) + (ids & 7)
            row = lax.broadcasted_iota(jnp.int32, (128, 128), 0)
            columns = pl.ds(pl.multiple_of(i * 128, 128), 128)
            lows[:, columns] = jnp.where(row == code, 1.0, 0.0).astype(BF)
            chunk = jnp.broadcast_to((ids >> 3) & 15, (16, 128))
            for k in range(16):
                hots[i, pl.ds(k * 16, 16)] = jnp.where(chunk == k, 1.0, 0.0).astype(BF)
            return carry

        lax.fori_loop(0, 16, body, 0)

    def contrib_start(j):
        upper = jnp.concatenate([high[j, 0], high[j, 1]], axis=1)
        lower = jnp.concatenate([low[j, 0], low[j, 1]], axis=1)
        value = dot(pick[...], upper)
        value = value[:128] + value[128:] + dot(pick[pl.ds(0, 128)], lower)
        contrib[j] = jnp.concatenate([value[:, :128].T, value[:, 128:].T], axis=0).reshape(16, 16, 128)
        spread[j, zone] = contrib[j, zone]
        for slot, device in others("zone"):
            pltpu.make_async_remote_copy(
                contrib.at[j, slot],
                spread.at[j, zone],
                well_send.at[j],
                well_recv.at[j],
                device_id=device,
                device_id_type=MESH,
            ).start()

    def dense_start(j):
        fifteen = spread.at[j, pl.ds(0, 15)]
        pltpu.make_async_copy(fifteen, fifteen, well_recv.at[j]).wait()

        def body(i, carry):
            upper, lower = split(spread[j, i])
            columns = pl.ds(pl.multiple_of(i * 128, 128), 128)
            hot = hots[i]
            placed[pl.ds(0, 256), columns] = jnp.concatenate([upper] * 16, axis=0) * hot
            placed[pl.ds(256, 256), columns] = jnp.concatenate([lower] * 16, axis=0) * hot
            return carry

        lax.fori_loop(0, 16, body, 0)
        total = lax.dot_general(
            placed[...], lows[...], (((1,), (1,)), ((), ())), preferred_element_type=F32
        )
        dense[j] = (total[:256] + total[256:]).reshape(32, 8, 128)
        partial[j, sub] = dense[j, sub]
        for slot, device in others("sub"):
            pltpu.make_async_remote_copy(
                dense.at[j, slot],
                partial.at[j, sub],
                well_send.at[4 + j],
                well_recv.at[4 + j],
                device_id=device,
                device_id_type=MESH,
            ).start()

    def dense_finish(j):
        most = partial.at[j, pl.ds(0, 31)]
        pltpu.make_async_copy(most, most, well_recv.at[4 + j]).wait()
        total = partial[j, 0]
        for i in range(1, 32):
            total = total + partial[j, i]
        _, me, _ = group("pair")
        final[j, me] = total
        for _, device in others("pair"):
            pltpu.make_async_remote_copy(
                final.at[j, me],
                final.at[j, me],
                well_send.at[7 + j],
                well_recv.at[7 + j],
                device_id=device,
                device_id_type=MESH,
            ).start()

    def own_wells(j):
        most = final.at[j, pl.ds(0, 31)]
        pltpu.make_async_copy(most, most, well_recv.at[7 + j]).wait()
        gathered = final[j].reshape(R, 128)
        turned[...] = jnp.concatenate([gathered[:128].T, gathered[128:].T], axis=1)
        eight = turned[pl.ds(pl.multiple_of(zone * 8, 8), 8)]
        return jnp.where(lax.rem(sub, 2) == 0, eight[:4], eight[4:])

    pick_build()
    loads[0].wait()
    loads[1].wait()
    for b in range(2):
        found = dot(pre[b], rhs[pl.ds(b * BLOCK, BLOCK)])
        for h in range(2):
            keep(0, h, b, found[:, h * 128 : h * 128 + 128])

    def right_side(h):
        return lambda rows: rhs[rows, pl.ds(h * 128, 128)].astype(F32)

    square = [inner_products([right_side(h)], [(0, 0)])[0] for h in range(2)]
    loads[2].wait()
    size_pre = largest_of(pre, 2)
    size_op = jnp.maximum(largest_of(diag, 2), OFF_MOST)
    pl.semaphore_wait(barrier, greeted)
    red_start(
        0,
        0,
        jnp.concatenate(
            square
            + [
                jnp.broadcast_to(size_pre, (1, 128)),
                jnp.broadcast_to(size_op, (1, 128)),
                jnp.zeros((4, 128), F32),
            ],
            axis=0,
        ),
    )
    halo_start(0, 0)
    halo_start(0, 1)
    wells_start()
    contrib_start(0)
    loads[3].wait()
    local_products(0, 0)
    local_products(0, 1)
    red_start(0, 1, red_finish(0, 0))
    for h in range(2):
        halo_products(0, h)
        precondition(1, h, None)
        halo_start(1, h)

    contrib_start(1)
    local_products(1, 0)
    red_start(0, 2, red_finish(0, 1))
    local_products(1, 1)
    lows_build()
    dense_start(0)
    scales = []

    def scale_of(h):
        def make():
            if not scales:
                sizes = red_finish(0, 2)
                norm = jnp.sqrt(sizes[:2])
                shrink = 1.0 / (sizes[2:3] * sizes[3:4])
                scales.extend([norm, shrink, 1.0 / norm])
            norm, shrink, inverse = scales
            return shrink * inverse[h : h + 1]

        return make

    for h in range(2):
        halo_products(1, h)
        precondition(2, h, scale_of(h))
        halo_start(2, h)

    norm, shrink, inverse = scales

    def makers(h, count):
        scale0 = inverse[h : h + 1]
        scale1 = shrink * scale0
        return [
            lambda rows: rhs[rows, pl.ds(h * 128, 128)].astype(F32) * scale0,
            lambda rows: image[0, h, rows] * scale0,
            lambda rows: image[1, h, rows] * scale1,
            lambda rows: image[2, h, rows] * shrink,
        ][:count]

    contrib_start(2)
    early = [
        inner_products(makers(h, 3), [(0, 1), (0, 2), (1, 1), (1, 2), (2, 2)]) for h in range(2)
    ]
    red_start(1, 0, payload(early, 16))
    local_products(2, 0)
    local_products(2, 1)
    dense_start(1)
    red_start(1, 1, red_finish(1, 0))
    dense_finish(0)
    late = []
    for h in range(2):
        halo_products(2, h)
        late.append(inner_products(makers(h, 4), [(0, 3), (1, 3), (2, 3), (3, 3)]))
    red_start(2, 0, payload(late, 8))
    dense_start(2)
    red_start(2, 1, red_finish(2, 0))
    red_start(1, 2, red_finish(1, 1))
    dense_finish(1)
    owned = [own_wells(0)]
    red_start(2, 2, red_finish(2, 1))
    head = red_finish(1, 2)
    g0, g1, m00, m01, m11 = [head[2 * i : 2 * i + 2] for i in range(5)]
    dense_finish(2)
    owned.append(own_wells(1))
    tail = red_finish(2, 2)
    g2, m02, m12, m22 = [tail[2 * i : 2 * i + 2] for i in range(4)]

    e01 = m01 / m00
    e02 = m02 / m00
    p11 = m11 - e01 * m01
    p12 = m12 - e01 * m02
    e12 = p12 / p11
    p22 = m22 - e02 * m02 - e12 * p12
    f0 = g0
    f1 = g1 - e01 * f0
    f2 = g2 - e02 * f0 - e12 * f1
    c2 = f2 / p22
    c1 = f1 / p11 - e12 * c2
    c0 = f0 / m00 - e01 * c1 - e02 * c2
    coeffs = [c0, c1 * shrink, c2 * shrink * norm]

    stores = []
    for part in range(4):
        rows = pl.ds(part * 192, 192)
        for h in range(2):
            total = coeffs[0][h : h + 1] * search[0, h, rows]
            for j in range(1, ITERS):
                total = total + coeffs[j][h : h + 1] * search[j, h, rows]
            out[rows, pl.ds(h * 128, 128)] = total
        store = pltpu.make_async_copy(out.at[rows], adj_hbm.at[rows], store_sem.at[part])
        store.start()
        stores.append(store)

    owned.append(own_wells(2))
    gradient = jnp.zeros((4, R), F32)
    for j in range(ITERS):
        wide = jnp.concatenate([coeffs[j][0:1], coeffs[j][1:2]], axis=1)
        gradient = gradient + wide * owned[j]
    grad_ref[...] = gradient

    for store in stores:
        store.wait()
    for j in range(ITERS):
        for h in range(2):
            for b in range(2):
                for kind in (SLOW, SIDE, FAST):
                    copy, sends, _ = halo(j, h, kind, b)
                    guarded(sends, copy.wait_send)
    for which in range(3):
        for stage in range(3):
            seven = reds[which].at[stage, pl.ds(0, 7)]
            pltpu.make_async_copy(seven, seven, red_send.at[which, stage]).wait()
    for j in range(ITERS):
        fifteen = spread.at[j, pl.ds(0, 15)]
        pltpu.make_async_copy(fifteen, fifteen, well_send.at[j]).wait()
        most = partial.at[j, pl.ds(0, 31)]
        pltpu.make_async_copy(most, most, well_send.at[4 + j]).wait()
        most = final.at[j, pl.ds(0, 31)]
        pltpu.make_async_copy(most, most, well_send.at[7 + j]).wait()
    fifteen = wells.at[pl.ds(0, 15)]
    pltpu.make_async_copy(fifteen, fifteen, well_send.at[3]).wait()


def shards(
    diag_blocks,
    precond_blocks,
    offdiag_blocks,
    offdiag_col,
    slot_live,
    adjoint_rhs,
    perf_cell,
    perf_well,
    perf_coeff,
):
    any_spec = pl.BlockSpec(memory_space=pl.ANY)
    smem = pl.BlockSpec(memory_space=pltpu.SMEM)
    vmem = pl.BlockSpec(memory_space=pltpu.VMEM)
    dma = pltpu.SemaphoreType.DMA
    adjoint, gradient = pl.pallas_call(
        kernel,
        out_shape=(
            jax.ShapeDtypeStruct((ROWS, R), F32),
            jax.ShapeDtypeStruct((4, R), F32),
        ),
        in_specs=[any_spec] * 4 + [smem] * 2 + [vmem] * 3,
        out_specs=(any_spec, vmem),
        scratch_shapes=[
            pltpu.VMEM((2, BLOCK, BLOCK), BF),
            pltpu.VMEM((2, BLOCK, BLOCK), BF),
            pltpu.VMEM((8, BLOCK, BLOCK), BF),
            pltpu.VMEM((ROWS, R), BF),
            pltpu.VMEM((ITERS, 2, ROWS, 128), F32),
            pltpu.VMEM((ITERS, 2, ROWS, 128), F32),
            pltpu.VMEM((ITERS, 2, ROWS, 128), BF),
            pltpu.VMEM((ITERS, 2, ROWS, 128), BF),
            pltpu.VMEM((ITERS, 2, 2, BLOCK, 128), BF),
            pltpu.VMEM((ITERS, 2, 2, BLOCK, 128), BF),
            pltpu.VMEM((ITERS, 2, 2, BLOCK, 128), BF),
            pltpu.VMEM((3, 8, 8, 128), F32),
            pltpu.VMEM((3, 8, 16, 128), F32),
            pltpu.VMEM((3, 8, 8, 128), F32),
            pltpu.VMEM((256, ROWS), BF),
            pltpu.VMEM((16, 1, 128), jnp.int32),
            pltpu.VMEM((128, 2048), BF),
            pltpu.VMEM((16, 256, 128), BF),
            pltpu.VMEM((ITERS, 16, 16, 128), F32),
            pltpu.VMEM((ITERS, 16, 16, 128), F32),
            pltpu.VMEM((512, 2048), BF),
            pltpu.VMEM((ITERS, 32, 8, 128), F32),
            pltpu.VMEM((ITERS, 32, 8, 128), F32),
            pltpu.VMEM((ITERS, 32, 8, 128), F32),
            pltpu.VMEM((128, R), F32),
            pltpu.VMEM((ROWS, R), F32),
            dma((4,)),
            dma((ITERS, 2, 6)),
            dma((ITERS, 2, 6)),
            dma((3, 3)),
            dma((3, 3)),
            dma((10,)),
            dma((10,)),
            dma((4,)),
        ],
        compiler_params=pltpu.CompilerParams(
            collective_id=0, has_side_effects=True, vmem_limit_bytes=60 * 1024 * 1024
        ),
        name="adjoint_solve",
    )(
        diag_blocks.reshape(2, BLOCK, BLOCK),
        precond_blocks.reshape(2, BLOCK, BLOCK),
        offdiag_blocks.reshape(8, BLOCK, BLOCK),
        adjoint_rhs.reshape(ROWS, R),
        offdiag_col.reshape(2, 4),
        slot_live.reshape(2, 4),
        perf_cell.reshape(1, 128),
        perf_well.reshape(1, 128),
        perf_coeff.reshape(3, 1, 128),
    )
    return adjoint.reshape(1, 1, 2, BLOCK, R), gradient


def solution(mesh):
    placed = (
        P("zone", "sub", None, None, None),
        P("zone", "sub", None, None, None),
        P("zone", "sub", None, None, None, None),
        P("zone", "sub", None, None),
        P("zone", "sub", None, None),
        P("zone", "sub", None, None, None),
        P("zone", "sub", None),
        P("zone", "sub", None),
        P("zone", "sub", None, None),
    )
    return jax.shard_map(
        shards,
        mesh=mesh,
        in_specs=placed,
        out_specs=(P("zone", "sub", None, None, None), P(("zone", "sub"), None)),
        check_vma=False,
    )
```

```python
import functools

import jax
import jax.numpy as jnp
from jax import lax
from jax.experimental import pallas as pl
from jax.experimental.pallas import tpu as pltpu
from jax.sharding import PartitionSpec as P

MESH = pl.DeviceIdType.MESH
BF = jnp.bfloat16
F32 = jnp.float32
BLOCK = 384
ROWS = 768
R = 256
ITERS = 3
OFF_MOST = 0.09375
FAST, SLOW, SIDE = 0, 2, 4
RED_ROWS = (8, 16, 8)


def place():
    zone = lax.axis_index("zone")
    sub = lax.axis_index("sub")
    return zone, sub, zone // 2, lax.rem(zone, 2), sub // 4, lax.rem(sub, 4)


def layout():
    _, _, y, core, z, x = place()
    twice = [2 * lax.rem(y + step, 8) for step in range(8)]
    cores = [core, 1 - core]
    layers = [lax.rem(z + step, 8) for step in range(8)]
    across = [lax.rem(x + step, 4) for step in range(4)]
    pair = [lax.rem(x, 2), 1 - lax.rem(x, 2)]
    aside = x - pair[0]
    one, two, four, eight = [(0,), (0, 1), range(4), range(8)]
    spans = {
        "xc": (one, two, one, four, lambda q, c, l, a: c * 4 + a),
        "y": (eight, one, one, one, lambda q, c, l, a: q // 2),
        "z": (one, one, eight, one, lambda q, c, l, a: l),
        "zone": (eight, two, one, one, lambda q, c, l, a: q + c),
        "sub": (one, one, eight, four, lambda q, c, l, a: l * 4 + a),
        "pair": (eight, two, one, two, lambda q, c, l, a: (q + c) * 2 + a),
    }
    groups = {}
    for name, (dys, dcs, dzs, dxs, slot_of) in spans.items():
        found = []
        for dy in dys:
            for dc in dcs:
                for dz in dzs:
                    for dx in dxs:
                        hops = min(dy, 8 - dy) + min(dz, 8 - dz) + min(dx, 4 - dx) + 0.4 * dc
                        a = pair[dx] if name == "pair" else across[dx]
                        slot = slot_of(twice[dy], cores[dc], layers[dz], a)
                        where = aside + a if name == "pair" else a
                        device = (twice[dy] + cores[dc], layers[dz] * 4 + where)
                        found.append((hops, slot, device))
        groups[name] = (found[0][1], [(slot, device) for hops, slot, device in sorted(found[1:], key=lambda e: -e[0])])
    return groups


def split(value):
    high = value.astype(BF)
    return high, (value - high.astype(F32)).astype(BF)


def dot(left, right):
    return jnp.dot(left, right, preferred_element_type=F32)


def kernel(
    diag_hbm,
    pre_hbm,
    off_hbm,
    rhs_hbm,
    col_hbm,
    live_hbm,
    cell_hbm,
    well_hbm,
    coeff_hbm,
    adj_ref,
    grad_ref,
    col_ref,
    live_ref,
    cell_ref,
    well_ref,
    coeff_ref,
    diag,
    pre,
    off,
    rhs,
    search,
    image,
    high,
    low,
    near,
    far,
    side,
    red0,
    red1,
    red2,
    pick,
    wells,
    lows,
    hots,
    contrib,
    spread,
    placed,
    dense,
    partial,
    final,
    turned,
    load_sem,
    halo_send,
    halo_recv,
    red_send,
    red_recv,
    well_send,
    well_recv,
):
    zone, sub, y, core, z, x = place()
    reds = (red0, red1, red2)
    groups = layout()

    def others(name):
        return groups[name][1]

    loads = [
        pltpu.make_async_copy(src, dst, load_sem.at[i])
        for i, (src, dst) in enumerate(
            (
                (pre_hbm, pre),
                (rhs_hbm, rhs),
                (diag_hbm, diag),
                (off_hbm, off),
                (cell_hbm, cell_ref),
                (coeff_hbm, coeff_ref),
                (well_hbm, well_ref),
                (col_hbm, col_ref),
                (live_hbm, live_ref),
            )
        )
    ]
    for load in loads:
        load.start()

    barrier = pltpu.get_barrier_semaphore()
    greeted = 0
    for name in ("zone", "sub", "pair", "xc"):
        for _, device in others(name):
            pl.semaphore_signal(barrier, inc=1, device_id=device, device_id_type=MESH)
            greeted += 1

    mate = (zone + 1 - 2 * core, sub)
    beyond = (zone - 1 + 2 * core, sub)
    has_far = jnp.logical_and(beyond[0] >= 0, beyond[0] < 16)
    has_side = (sub > 0, sub < 31)
    side_dev = ((zone, sub - 1), (zone, sub + 1))

    @pl.when(jnp.logical_not(has_far))
    def _():
        far[...] = jnp.zeros(far.shape, BF)

    for b in range(2):

        @pl.when(jnp.logical_not(has_side[b]))
        def _():
            side[:, :, b] = jnp.zeros((ITERS, 2, BLOCK, 128), BF)

    def halo(j, h, kind, b):
        src = high.at[j, h, pl.ds(b * BLOCK, BLOCK)]
        dst, device, sends, receives = {
            SIDE: (side.at[j, h, 1 - b], side_dev[b], has_side[b], has_side[1 - b]),
            SLOW: (far.at[j, h, b], beyond, has_far, has_far),
            FAST: (near.at[j, h, b], mate, None, None),
        }[kind]
        copy = pltpu.make_async_remote_copy(
            src,
            dst,
            halo_send.at[j, h, kind + b],
            halo_recv.at[j, h, kind + b],
            device_id=device,
            device_id_type=MESH,
        )
        return copy, sends, receives

    def guarded(condition, action):
        if condition is None:
            action()
        else:
            pl.when(condition)(action)

    def halo_start(j, h):
        for b in range(2):
            for kind in (SLOW, SIDE, FAST):
                copy, sends, _ = halo(j, h, kind, b)
                guarded(sends, copy.start)

    def halo_wait(j, h, kind):
        for b in range(2):
            copy, _, receives = halo(j, h, kind, b)
            guarded(receives, copy.wait_recv)

    def keep(j, h, b, found):
        rows = pl.ds(b * BLOCK, BLOCK)
        search[j, h, rows] = found
        upper, lower = split(found)
        high[j, h, rows] = upper
        low[j, h, rows] = lower

    def both(left, upper, lower):
        found = dot(left, jnp.concatenate([upper, lower], axis=1))
        return found[:, :128] + found[:, 128:]

    def precondition(j, h, scale):
        for b in range(2):
            upper, lower = split(image[j - 1, h, pl.ds(b * BLOCK, BLOCK)])
            found = both(pre[b], upper, lower)
            keep(j, h, b, found if scale is None else found * scale())

    def slot_of(b, position):
        where = 0
        for k in range(1, 4):
            where = where + jnp.where(col_ref[b, k] == position, k, 0)
        return b * 4 + where

    def live_of(b, position):
        found = 0
        for k in range(4):
            found = found + jnp.where(col_ref[b, k] == position, live_ref[b, k], 0)
        return found

    def local_products(j, h):
        for b in range(2):
            mine = pl.ds(b * BLOCK, BLOCK)
            other = pl.ds((1 - b) * BLOCK, BLOCK)
            total = both(diag[b], high[j, h, mine], low[j, h, mine])
            inner = both(off[slot_of(b, 6 - b)], high[j, h, other], low[j, h, other])
            image[j, h, mine] = total + jnp.where(live_of(b, 6 - b) > 0, inner, 0.0)

    def halo_products(j, h):
        def add(b, position, block):
            image[j, h, pl.ds(b * BLOCK, BLOCK)] += dot(off[slot_of(b, position)], block)

        halo_wait(j, h, FAST)
        for b in range(2):
            add(b, jnp.where(core == 0, 9 + b, 1 + b), near[j, h, b])
        halo_wait(j, h, SIDE)
        for b in range(2):
            add(b, 4 + 3 * b, side[j, h, b])
        halo_wait(j, h, SLOW)
        for b in range(2):
            add(b, jnp.where(core == 0, 1 + b, 9 + b), far[j, h, b])

    stages = ("xc", "y", "z")

    def red_start(which, stage, value):
        buf = reds[which].at[stage]
        me = groups[stages[stage]][0]
        buf[me] = value
        for _, device in others(stages[stage]):
            pltpu.make_async_remote_copy(
                buf.at[me],
                buf.at[me],
                red_send.at[which, stage],
                red_recv.at[which, stage],
                device_id=device,
                device_id_type=MESH,
            ).start()

    def red_finish(which, stage):
        buf = reds[which].at[stage]
        seven = buf.at[pl.ds(0, 7)]
        pltpu.make_async_copy(seven, seven, red_recv.at[which, stage]).wait()
        total = buf[0]
        for i in range(1, 8):
            total = total + buf[i]
        if which == 0:
            largest = buf[0]
            for i in range(1, 8):
                largest = jnp.maximum(largest, buf[i])
            row = lax.broadcasted_iota(jnp.int32, total.shape, 0)
            total = jnp.where(row < 2, total, largest)
        return total

    def inner_products(makers, pairs):
        step = 128

        def body(i, sums):
            rows = pl.ds(pl.multiple_of(i * step, step), step)
            vectors = [make(rows) for make in makers]
            return tuple(
                total + jnp.sum((vectors[a] * vectors[c]).reshape(step // 8, 8, 128), axis=0)
                for total, (a, c) in zip(sums, pairs)
            )

        sums = lax.fori_loop(
            0, ROWS // step, body, tuple(jnp.zeros((8, 128), F32) for _ in pairs)
        )
        return [jnp.sum(total, axis=0, keepdims=True) for total in sums]

    def payload(values, rows):
        pieces = [half for pair in zip(*values) for half in pair]
        if len(pieces) < rows:
            pieces.append(jnp.zeros((rows - len(pieces), 128), F32))
        return jnp.concatenate(pieces, axis=0)

    def largest_of(ref, count):
        def body(i, best):
            return jnp.maximum(best, jnp.max(jnp.abs(ref[i].astype(F32).reshape(48, 8, BLOCK)), axis=0))

        best = lax.fori_loop(0, count, body, jnp.zeros((8, BLOCK), F32))
        return jnp.max(jnp.max(best, axis=0, keepdims=True), axis=1, keepdims=True)

    def wells_start():
        wells[zone] = well_ref[...]
        for _, device in others("zone"):
            pltpu.make_async_remote_copy(
                wells.at[zone],
                wells.at[zone],
                well_send.at[3],
                well_recv.at[3],
                device_id=device,
                device_id_type=MESH,
            ).start()

    def pick_build():
        cells = cell_ref[...]
        for b in range(2):
            for q in range(3):
                row = lax.broadcasted_iota(jnp.int32, (128, 128), 0) + b * 128
                upper, lower = split(jnp.where(row == cells, -coeff_ref[q], 0.0).T)
                columns = pl.ds(b * BLOCK + q * 128, 128)
                pick[pl.ds(0, 128), columns] = upper
                pick[pl.ds(128, 128), columns] = lower

    def lows_build():
        fifteen = wells.at[pl.ds(0, 15)]
        pltpu.make_async_copy(fifteen, fifteen, well_recv.at[3]).wait()

        def body(i, carry):
            ids = wells[i]
            code = ((ids >> 7) << 3) + (ids & 7)
            row = lax.broadcasted_iota(jnp.int32, (128, 128), 0)
            columns = pl.ds(pl.multiple_of(i * 128, 128), 128)
            lows[:, columns] = jnp.where(row == code, 1.0, 0.0).astype(BF)
            chunk = jnp.broadcast_to((ids >> 3) & 15, (16, 128))
            for k in range(16):
                hots[i, pl.ds(k * 16, 16)] = jnp.where(chunk == k, 1.0, 0.0).astype(BF)
            return carry

        lax.fori_loop(0, 16, body, 0)

    def contrib_start(j):
        upper = jnp.concatenate([high[j, 0], high[j, 1]], axis=1)
        lower = jnp.concatenate([low[j, 0], low[j, 1]], axis=1)
        value = dot(pick[...], upper)
        value = value[:128] + value[128:] + dot(pick[pl.ds(0, 128)], lower)
        contrib[j] = jnp.concatenate([value[:, :128].T, value[:, 128:].T], axis=0).reshape(16, 16, 128)
        spread[j, zone] = contrib[j, zone]
        for slot, device in others("zone"):
            pltpu.make_async_remote_copy(
                contrib.at[j, slot],
                spread.at[j, zone],
                well_send.at[j],
                well_recv.at[j],
                device_id=device,
                device_id_type=MESH,
            ).start()

    def dense_start(j):
        fifteen = spread.at[j, pl.ds(0, 15)]
        pltpu.make_async_copy(fifteen, fifteen, well_recv.at[j]).wait()

        def body(i, carry):
            upper, lower = split(spread[j, i])
            columns = pl.ds(pl.multiple_of(i * 128, 128), 128)
            hot = hots[i]
            placed[pl.ds(0, 256), columns] = jnp.concatenate([upper] * 16, axis=0) * hot
            placed[pl.ds(256, 256), columns] = jnp.concatenate([lower] * 16, axis=0) * hot
            return carry

        lax.fori_loop(0, 16, body, 0)
        total = lax.dot_general(
            placed[...], lows[...], (((1,), (1,)), ((), ())), preferred_element_type=F32
        )
        dense[j] = (total[:256] + total[256:]).reshape(32, 8, 128)
        partial[j, sub] = dense[j, sub]
        for slot, device in others("sub"):
            pltpu.make_async_remote_copy(
                dense.at[j, slot],
                partial.at[j, sub],
                well_send.at[4 + j],
                well_recv.at[4 + j],
                device_id=device,
                device_id_type=MESH,
            ).start()

    def dense_finish(j):
        most = partial.at[j, pl.ds(0, 31)]
        pltpu.make_async_copy(most, most, well_recv.at[4 + j]).wait()
        total = partial[j, 0]
        for i in range(1, 32):
            total = total + partial[j, i]
        me = groups["pair"][0]
        final[j, me] = total
        for _, device in others("pair"):
            pltpu.make_async_remote_copy(
                final.at[j, me],
                final.at[j, me],
                well_send.at[7 + j],
                well_recv.at[7 + j],
                device_id=device,
                device_id_type=MESH,
            ).start()

    def own_wells(j):
        most = final.at[j, pl.ds(0, 31)]
        pltpu.make_async_copy(most, most, well_recv.at[7 + j]).wait()
        gathered = final[j].reshape(R, 128)
        turned[...] = jnp.concatenate([gathered[:128].T, gathered[128:].T], axis=1)
        eight = turned[pl.ds(pl.multiple_of(zone * 8, 8), 8)]
        return jnp.where(lax.rem(sub, 2) == 0, eight[:4], eight[4:])

    loads[4].wait()
    loads[5].wait()
    pick_build()
    loads[0].wait()
    loads[1].wait()
    for b in range(2):
        found = dot(pre[b], rhs[pl.ds(b * BLOCK, BLOCK)])
        for h in range(2):
            keep(0, h, b, found[:, h * 128 : h * 128 + 128])

    def right_side(h):
        return lambda rows: rhs[rows, pl.ds(h * 128, 128)].astype(F32)

    square = [inner_products([right_side(h)], [(0, 0)])[0] for h in range(2)]
    loads[2].wait()
    size_pre = largest_of(pre, 2)
    size_op = jnp.maximum(largest_of(diag, 2), OFF_MOST)
    pl.semaphore_wait(barrier, greeted)
    red_start(
        0,
        0,
        jnp.concatenate(
            square
            + [
                jnp.broadcast_to(size_pre, (1, 128)),
                jnp.broadcast_to(size_op, (1, 128)),
                jnp.zeros((4, 128), F32),
            ],
            axis=0,
        ),
    )
    halo_start(0, 0)
    halo_start(0, 1)
    loads[6].wait()
    wells_start()
    contrib_start(0)
    loads[3].wait()
    loads[7].wait()
    loads[8].wait()
    local_products(0, 0)
    local_products(0, 1)
    red_start(0, 1, red_finish(0, 0))
    for h in range(2):
        halo_products(0, h)
        precondition(1, h, None)
        halo_start(1, h)

    contrib_start(1)
    local_products(1, 0)
    red_start(0, 2, red_finish(0, 1))
    local_products(1, 1)
    lows_build()
    dense_start(0)
    scales = []

    def scale_of(h):
        def make():
            if not scales:
                sizes = red_finish(0, 2)
                norm = jnp.sqrt(sizes[:2])
                shrink = 1.0 / (sizes[2:3] * sizes[3:4])
                scales.extend([norm, shrink, 1.0 / norm])
            norm, shrink, inverse = scales
            return shrink * inverse[h : h + 1]

        return make

    for h in range(2):
        halo_products(1, h)
        precondition(2, h, scale_of(h))
        halo_start(2, h)

    norm, shrink, inverse = scales

    def makers(h, count):
        scale0 = inverse[h : h + 1]
        scale1 = shrink * scale0
        return [
            lambda rows: rhs[rows, pl.ds(h * 128, 128)].astype(F32) * scale0,
            lambda rows: image[0, h, rows] * scale0,
            lambda rows: image[1, h, rows] * scale1,
            lambda rows: image[2, h, rows] * shrink,
        ][:count]

    contrib_start(2)
    early = [
        inner_products(makers(h, 3), [(0, 1), (0, 2), (1, 1), (1, 2), (2, 2)]) for h in range(2)
    ]
    red_start(1, 0, payload(early, 16))
    local_products(2, 0)
    local_products(2, 1)
    dense_start(1)
    red_start(1, 1, red_finish(1, 0))
    dense_finish(0)
    late = []
    for h in range(2):
        halo_products(2, h)
        late.append(inner_products(makers(h, 4), [(0, 3), (1, 3), (2, 3), (3, 3)]))
    red_start(2, 0, payload(late, 8))
    dense_start(2)
    red_start(2, 1, red_finish(2, 0))
    red_start(1, 2, red_finish(1, 1))
    dense_finish(1)
    owned = [own_wells(0)]
    red_start(2, 2, red_finish(2, 1))
    head = red_finish(1, 2)
    g0, g1, m00, m01, m11 = [head[2 * i : 2 * i + 2] for i in range(5)]
    dense_finish(2)
    owned.append(own_wells(1))
    tail = red_finish(2, 2)
    g2, m02, m12, m22 = [tail[2 * i : 2 * i + 2] for i in range(4)]

    e01 = m01 / m00
    e02 = m02 / m00
    p11 = m11 - e01 * m01
    p12 = m12 - e01 * m02
    e12 = p12 / p11
    p22 = m22 - e02 * m02 - e12 * p12
    f0 = g0
    f1 = g1 - e01 * f0
    f2 = g2 - e02 * f0 - e12 * f1
    c2 = f2 / p22
    c1 = f1 / p11 - e12 * c2
    c0 = f0 / m00 - e01 * c1 - e02 * c2
    coeffs = [c0, c1 * shrink, c2 * shrink * norm]

    for part in range(4):
        rows = pl.ds(part * 192, 192)
        for h in range(2):
            total = coeffs[0][h : h + 1] * search[0, h, rows]
            for j in range(1, ITERS):
                total = total + coeffs[j][h : h + 1] * search[j, h, rows]
            adj_ref[rows, pl.ds(h * 128, 128)] = total

    owned.append(own_wells(2))
    gradient = jnp.zeros((4, R), F32)
    for j in range(ITERS):
        wide = jnp.concatenate([coeffs[j][0:1], coeffs[j][1:2]], axis=1)
        gradient = gradient + wide * owned[j]
    grad_ref[...] = gradient

    for j in range(ITERS):
        for h in range(2):
            for b in range(2):
                for kind in (SLOW, SIDE, FAST):
                    copy, sends, _ = halo(j, h, kind, b)
                    guarded(sends, copy.wait_send)
    for which in range(3):
        for stage in range(3):
            seven = reds[which].at[stage, pl.ds(0, 7)]
            pltpu.make_async_copy(seven, seven, red_send.at[which, stage]).wait()
    for j in range(ITERS):
        fifteen = spread.at[j, pl.ds(0, 15)]
        pltpu.make_async_copy(fifteen, fifteen, well_send.at[j]).wait()
        most = partial.at[j, pl.ds(0, 31)]
        pltpu.make_async_copy(most, most, well_send.at[4 + j]).wait()
        most = final.at[j, pl.ds(0, 31)]
        pltpu.make_async_copy(most, most, well_send.at[7 + j]).wait()
    fifteen = wells.at[pl.ds(0, 15)]
    pltpu.make_async_copy(fifteen, fifteen, well_send.at[3]).wait()


def shards(
    diag_blocks,
    precond_blocks,
    offdiag_blocks,
    offdiag_col,
    slot_live,
    adjoint_rhs,
    perf_cell,
    perf_well,
    perf_coeff,
):
    any_spec = pl.BlockSpec(memory_space=pl.ANY)
    vmem = pl.BlockSpec(memory_space=pltpu.VMEM)
    dma = pltpu.SemaphoreType.DMA
    adjoint, gradient = pl.pallas_call(
        kernel,
        out_shape=(
            pltpu.VMEM((ROWS, R), F32),
            pltpu.VMEM((4, R), F32),
        ),
        in_specs=[any_spec] * 9,
        out_specs=(vmem, vmem),
        scratch_shapes=[
            pltpu.SMEM((2, 4), jnp.int32),
            pltpu.SMEM((2, 4), jnp.int32),
            pltpu.VMEM((1, 128), jnp.int32),
            pltpu.VMEM((1, 128), jnp.int32),
            pltpu.VMEM((3, 1, 128), F32),
            pltpu.VMEM((2, BLOCK, BLOCK), BF),
            pltpu.VMEM((2, BLOCK, BLOCK), BF),
            pltpu.VMEM((8, BLOCK, BLOCK), BF),
            pltpu.VMEM((ROWS, R), BF),
            pltpu.VMEM((ITERS, 2, ROWS, 128), F32),
            pltpu.VMEM((ITERS, 2, ROWS, 128), F32),
            pltpu.VMEM((ITERS, 2, ROWS, 128), BF),
            pltpu.VMEM((ITERS, 2, ROWS, 128), BF),
            pltpu.VMEM((ITERS, 2, 2, BLOCK, 128), BF),
            pltpu.VMEM((ITERS, 2, 2, BLOCK, 128), BF),
            pltpu.VMEM((ITERS, 2, 2, BLOCK, 128), BF),
            pltpu.VMEM((3, 8, 8, 128), F32),
            pltpu.VMEM((3, 8, 16, 128), F32),
            pltpu.VMEM((3, 8, 8, 128), F32),
            pltpu.VMEM((256, ROWS), BF),
            pltpu.VMEM((16, 1, 128), jnp.int32),
            pltpu.VMEM((128, 2048), BF),
            pltpu.VMEM((16, 256, 128), BF),
            pltpu.VMEM((ITERS, 16, 16, 128), F32),
            pltpu.VMEM((ITERS, 16, 16, 128), F32),
            pltpu.VMEM((512, 2048), BF),
            pltpu.VMEM((ITERS, 32, 8, 128), F32),
            pltpu.VMEM((ITERS, 32, 8, 128), F32),
            pltpu.VMEM((ITERS, 32, 8, 128), F32),
            pltpu.VMEM((128, R), F32),
            dma((9,)),
            dma((ITERS, 2, 6)),
            dma((ITERS, 2, 6)),
            dma((3, 3)),
            dma((3, 3)),
            dma((10,)),
            dma((10,)),
        ],
        compiler_params=pltpu.CompilerParams(
            collective_id=0, has_side_effects=True, vmem_limit_bytes=60 * 1024 * 1024
        ),
        name="adjoint_solve",
    )(
        diag_blocks.reshape(2, BLOCK, BLOCK),
        precond_blocks.reshape(2, BLOCK, BLOCK),
        offdiag_blocks.reshape(8, BLOCK, BLOCK),
        adjoint_rhs.reshape(ROWS, R),
        offdiag_col.reshape(2, 4),
        slot_live.reshape(2, 4),
        perf_cell.reshape(1, 128),
        perf_well.reshape(1, 128),
        perf_coeff.reshape(3, 1, 128),
    )
    return adjoint.reshape(1, 1, 2, BLOCK, R), gradient


def solution(mesh):
    placed = (
        P("zone", "sub", None, None, None),
        P("zone", "sub", None, None, None),
        P("zone", "sub", None, None, None, None),
        P("zone", "sub", None, None),
        P("zone", "sub", None, None),
        P("zone", "sub", None, None, None),
        P("zone", "sub", None),
        P("zone", "sub", None),
        P("zone", "sub", None, None),
    )
    return jax.shard_map(
        shards,
        mesh=mesh,
        in_specs=placed,
        out_specs=(P("zone", "sub", None, None, None), P(("zone", "sub"), None)),
        check_vma=False,
    )
```

```python
import functools

import jax
import jax.numpy as jnp
from jax import lax
from jax.experimental import pallas as pl
from jax.experimental.pallas import tpu as pltpu
from jax.sharding import PartitionSpec as P

MESH = pl.DeviceIdType.MESH
BF = jnp.bfloat16
F32 = jnp.float32
BLOCK = 384
ROWS = 768
R = 256
ITERS = 3
OFF_MOST = 0.09375
ALPHA = 2.0**-12
FAST, SLOW, SIDE = 0, 2, 4


def place():
    zone = lax.axis_index("zone")
    sub = lax.axis_index("sub")
    return zone, sub, zone // 2, lax.rem(zone, 2), sub // 4, lax.rem(sub, 4)


def layout():
    _, _, y, core, z, x = place()
    twice = [2 * lax.rem(y + step, 8) for step in range(8)]
    cores = [core, 1 - core]
    layers = [lax.rem(z + step, 8) for step in range(8)]
    across = [lax.rem(x + step, 4) for step in range(4)]
    pair = [lax.rem(x, 2), 1 - lax.rem(x, 2)]
    aside = x - pair[0]
    one, two, four, eight = [(0,), (0, 1), range(4), range(8)]
    spans = {
        "xc": (one, two, one, four, lambda q, c, l, a: c * 4 + a),
        "y": (eight, one, one, one, lambda q, c, l, a: q // 2),
        "z": (one, one, eight, one, lambda q, c, l, a: l),
        "zone": (eight, two, one, one, lambda q, c, l, a: q + c),
        "sub": (one, one, eight, four, lambda q, c, l, a: l * 4 + a),
        "pair": (eight, two, one, two, lambda q, c, l, a: (q + c) * 2 + a),
    }
    groups = {}
    for name, (dys, dcs, dzs, dxs, slot_of) in spans.items():
        found = []
        for dy in dys:
            for dc in dcs:
                for dz in dzs:
                    for dx in dxs:
                        hops = min(dy, 8 - dy) + min(dz, 8 - dz) + min(dx, 4 - dx) + 0.4 * dc
                        a = pair[dx] if name == "pair" else across[dx]
                        slot = slot_of(twice[dy], cores[dc], layers[dz], a)
                        where = aside + a if name == "pair" else a
                        device = (twice[dy] + cores[dc], layers[dz] * 4 + where)
                        found.append((hops, slot, device))
        groups[name] = (found[0][1], [(slot, device) for hops, slot, device in sorted(found[1:], key=lambda e: -e[0])])
    return groups


def split(value):
    high = value.astype(BF)
    return high, (value - high.astype(F32)).astype(BF)


def dot(left, right):
    return jnp.dot(left, right, preferred_element_type=F32)


def kernel(
    diag_hbm,
    pre_hbm,
    off_hbm,
    rhs_hbm,
    col_hbm,
    live_hbm,
    cell_hbm,
    well_hbm,
    coeff_hbm,
    adj_ref,
    grad_ref,
    col_ref,
    live_ref,
    cell_ref,
    well_ref,
    coeff_ref,
    diag,
    pre,
    off,
    rhs,
    search,
    image,
    high,
    low,
    near,
    far,
    side,
    size0,
    size1,
    red1,
    red2,
    pick,
    wells,
    lows,
    hots,
    contrib,
    spread,
    placed,
    dense,
    partial,
    final,
    turned,
    load_sem,
    halo_send,
    halo_recv,
    red_send,
    red_recv,
    well_send,
    well_recv,
):
    zone, sub, y, core, z, x = place()
    sizes = (size0, size1)
    reds = (red1, red2)
    groups = layout()

    def others(name):
        return groups[name][1]

    loads = [
        pltpu.make_async_copy(src, dst, load_sem.at[i])
        for i, (src, dst) in enumerate(
            (
                (pre_hbm, pre),
                (rhs_hbm, rhs),
                (diag_hbm, diag),
                (off_hbm, off),
                (cell_hbm, cell_ref),
                (coeff_hbm, coeff_ref),
                (well_hbm, well_ref),
                (col_hbm, col_ref),
                (live_hbm, live_ref),
            )
        )
    ]
    for load in loads:
        load.start()

    barrier = pltpu.get_barrier_semaphore()
    greeted = 0
    for name in ("zone", "sub", "pair", "xc"):
        for _, device in others(name):
            pl.semaphore_signal(barrier, inc=1, device_id=device, device_id_type=MESH)
            greeted += 1

    mate = (zone + 1 - 2 * core, sub)
    beyond = (zone - 1 + 2 * core, sub)
    has_far = jnp.logical_and(beyond[0] >= 0, beyond[0] < 16)
    has_side = (sub > 0, sub < 31)
    side_dev = ((zone, sub - 1), (zone, sub + 1))

    @pl.when(jnp.logical_not(has_far))
    def _():
        far[...] = jnp.zeros(far.shape, BF)

    for b in range(2):

        @pl.when(jnp.logical_not(has_side[b]))
        def _():
            side[:, :, b] = jnp.zeros((ITERS, 2, BLOCK, 128), BF)

    def halo(j, h, kind, b):
        src = high.at[j, h, pl.ds(b * BLOCK, BLOCK)]
        dst, device, sends, receives = {
            SIDE: (side.at[j, h, 1 - b], side_dev[b], has_side[b], has_side[1 - b]),
            SLOW: (far.at[j, h, b], beyond, has_far, has_far),
            FAST: (near.at[j, h, b], mate, None, None),
        }[kind]
        copy = pltpu.make_async_remote_copy(
            src,
            dst,
            halo_send.at[j, h, kind + b],
            halo_recv.at[j, h, kind + b],
            device_id=device,
            device_id_type=MESH,
        )
        return copy, sends, receives

    def guarded(condition, action):
        if condition is None:
            action()
        else:
            pl.when(condition)(action)

    def halo_start(j, h):
        for b in range(2):
            for kind in (SLOW, SIDE, FAST):
                copy, sends, _ = halo(j, h, kind, b)
                guarded(sends, copy.start)

    def halo_wait(j, h, kind):
        for b in range(2):
            copy, _, receives = halo(j, h, kind, b)
            guarded(receives, copy.wait_recv)

    def keep(j, h, b, found):
        rows = pl.ds(b * BLOCK, BLOCK)
        search[j, h, rows] = found
        upper, lower = split(found)
        high[j, h, rows] = upper
        low[j, h, rows] = lower

    def both(left, upper, lower):
        found = dot(left, jnp.concatenate([upper, lower], axis=1))
        return found[:, :128] + found[:, 128:]

    def precondition(j, h, scale):
        for b in range(2):
            upper, lower = split(image[j - 1, h, pl.ds(b * BLOCK, BLOCK)])
            found = both(pre[b], upper, lower)
            keep(j, h, b, found if scale is None else found * scale())

    def slot_of(b, position):
        where = 0
        for k in range(1, 4):
            where = where + jnp.where(col_ref[b, k] == position, k, 0)
        return b * 4 + where

    def live_of(b, position):
        found = 0
        for k in range(4):
            found = found + jnp.where(col_ref[b, k] == position, live_ref[b, k], 0)
        return found

    def local_products(j, h):
        for b in range(2):
            mine = pl.ds(b * BLOCK, BLOCK)
            other = pl.ds((1 - b) * BLOCK, BLOCK)
            total = both(diag[b], high[j, h, mine], low[j, h, mine])
            inner = both(off[slot_of(b, 6 - b)], high[j, h, other], low[j, h, other])
            image[j, h, mine] = total + jnp.where(live_of(b, 6 - b) > 0, inner, 0.0)

    def halo_products(j, h):
        def add(b, position, block):
            image[j, h, pl.ds(b * BLOCK, BLOCK)] += dot(off[slot_of(b, position)], block)

        halo_wait(j, h, FAST)
        for b in range(2):
            add(b, jnp.where(core == 0, 9 + b, 1 + b), near[j, h, b])
        halo_wait(j, h, SIDE)
        for b in range(2):
            add(b, 4 + 3 * b, side[j, h, b])
        halo_wait(j, h, SLOW)
        for b in range(2):
            add(b, jnp.where(core == 0, 1 + b, 9 + b), far[j, h, b])

    stages = ("xc", "y", "z")

    def red_start(which, stage, value):
        buf = reds[which].at[stage]
        me = groups[stages[stage]][0]
        buf[me] = value
        for _, device in others(stages[stage]):
            pltpu.make_async_remote_copy(
                buf.at[me],
                buf.at[me],
                red_send.at[which, stage],
                red_recv.at[which, stage],
                device_id=device,
                device_id_type=MESH,
            ).start()

    def red_finish(which, stage):
        buf = reds[which].at[stage]
        seven = buf.at[pl.ds(0, 7)]
        pltpu.make_async_copy(seven, seven, red_recv.at[which, stage]).wait()
        total = buf[0]
        for i in range(1, 8):
            total = total + buf[i]
        return total

    def size_start(stage, value):
        name = ("zone", "sub")[stage]
        buf = sizes[stage]
        me = groups[name][0]
        buf[me] = value
        for _, device in others(name):
            pltpu.make_async_remote_copy(
                buf.at[me],
                buf.at[me],
                red_send.at[2, stage],
                red_recv.at[2, stage],
                device_id=device,
                device_id_type=MESH,
            ).start()

    def size_finish(stage):
        buf = sizes[stage]
        count = buf.shape[0]
        rest = buf.at[pl.ds(0, count - 1)]
        pltpu.make_async_copy(rest, rest, red_recv.at[2, stage]).wait()
        total = buf[0]
        for i in range(1, count):
            total = jnp.maximum(total, buf[i])
        return total

    def inner_products(makers, pairs):
        step = 128

        def body(i, sums):
            rows = pl.ds(pl.multiple_of(i * step, step), step)
            vectors = [make(rows) for make in makers]
            return tuple(
                total + jnp.sum((vectors[a] * vectors[c]).reshape(step // 8, 8, 128), axis=0)
                for total, (a, c) in zip(sums, pairs)
            )

        sums = lax.fori_loop(
            0, ROWS // step, body, tuple(jnp.zeros((8, 128), F32) for _ in pairs)
        )
        return [jnp.sum(total, axis=0, keepdims=True) for total in sums]

    def payload(values, rows):
        pieces = [half for pair in zip(*values) for half in pair]
        if len(pieces) < rows:
            pieces.append(jnp.zeros((rows - len(pieces), 128), F32))
        return jnp.concatenate(pieces, axis=0)

    def largest_of(ref, count):
        def body(i, best):
            return jnp.maximum(best, jnp.max(jnp.abs(ref[i].astype(F32).reshape(48, 8, BLOCK)), axis=0))

        best = lax.fori_loop(0, count, body, jnp.zeros((8, BLOCK), F32))
        return jnp.max(jnp.max(best, axis=0, keepdims=True), axis=1, keepdims=True)

    def wells_start():
        wells[zone] = well_ref[...]
        for _, device in others("zone"):
            pltpu.make_async_remote_copy(
                wells.at[zone],
                wells.at[zone],
                well_send.at[3],
                well_recv.at[3],
                device_id=device,
                device_id_type=MESH,
            ).start()

    def pick_build():
        cells = cell_ref[...]
        for b in range(2):
            for q in range(3):
                row = lax.broadcasted_iota(jnp.int32, (128, 128), 0) + b * 128
                upper, lower = split(jnp.where(row == cells, -coeff_ref[q], 0.0).T)
                columns = pl.ds(b * BLOCK + q * 128, 128)
                pick[pl.ds(0, 128), columns] = upper
                pick[pl.ds(128, 128), columns] = lower

    def lows_build():
        fifteen = wells.at[pl.ds(0, 15)]
        pltpu.make_async_copy(fifteen, fifteen, well_recv.at[3]).wait()

        def body(i, carry):
            ids = wells[i]
            code = ((ids >> 7) << 3) + (ids & 7)
            row = lax.broadcasted_iota(jnp.int32, (128, 128), 0)
            columns = pl.ds(pl.multiple_of(i * 128, 128), 128)
            lows[:, columns] = jnp.where(row == code, 1.0, 0.0).astype(BF)
            chunk = jnp.broadcast_to((ids >> 3) & 15, (16, 128))
            for k in range(16):
                hots[i, pl.ds(k * 16, 16)] = jnp.where(chunk == k, 1.0, 0.0).astype(BF)
            return carry

        lax.fori_loop(0, 16, body, 0)

    def contrib_start(j):
        upper = jnp.concatenate([high[j, 0], high[j, 1]], axis=1)
        lower = jnp.concatenate([low[j, 0], low[j, 1]], axis=1)
        value = dot(pick[...], upper)
        value = value[:128] + value[128:] + dot(pick[pl.ds(0, 128)], lower)
        contrib[j] = jnp.concatenate([value[:, :128].T, value[:, 128:].T], axis=0).reshape(16, 16, 128)
        spread[j, zone] = contrib[j, zone]
        for slot, device in others("zone"):
            pltpu.make_async_remote_copy(
                contrib.at[j, slot],
                spread.at[j, zone],
                well_send.at[j],
                well_recv.at[j],
                device_id=device,
                device_id_type=MESH,
            ).start()

    def dense_start(j):
        fifteen = spread.at[j, pl.ds(0, 15)]
        pltpu.make_async_copy(fifteen, fifteen, well_recv.at[j]).wait()

        def body(i, carry):
            upper, lower = split(spread[j, i])
            columns = pl.ds(pl.multiple_of(i * 128, 128), 128)
            hot = hots[i]
            placed[pl.ds(0, 256), columns] = jnp.concatenate([upper] * 16, axis=0) * hot
            placed[pl.ds(256, 256), columns] = jnp.concatenate([lower] * 16, axis=0) * hot
            return carry

        lax.fori_loop(0, 16, body, 0)
        total = lax.dot_general(
            placed[...], lows[...], (((1,), (1,)), ((), ())), preferred_element_type=F32
        )
        dense[j] = (total[:256] + total[256:]).reshape(32, 8, 128)
        partial[j, sub] = dense[j, sub]
        for slot, device in others("sub"):
            pltpu.make_async_remote_copy(
                dense.at[j, slot],
                partial.at[j, sub],
                well_send.at[4 + j],
                well_recv.at[4 + j],
                device_id=device,
                device_id_type=MESH,
            ).start()

    def dense_finish(j):
        most = partial.at[j, pl.ds(0, 31)]
        pltpu.make_async_copy(most, most, well_recv.at[4 + j]).wait()
        total = partial[j, 0]
        for i in range(1, 32):
            total = total + partial[j, i]
        me = groups["pair"][0]
        final[j, me] = total
        for _, device in others("pair"):
            pltpu.make_async_remote_copy(
                final.at[j, me],
                final.at[j, me],
                well_send.at[7 + j],
                well_recv.at[7 + j],
                device_id=device,
                device_id_type=MESH,
            ).start()

    def own_wells(j):
        most = final.at[j, pl.ds(0, 31)]
        pltpu.make_async_copy(most, most, well_recv.at[7 + j]).wait()
        gathered = final[j].reshape(R, 128)
        turned[...] = jnp.concatenate([gathered[:128].T, gathered[128:].T], axis=1)
        eight = turned[pl.ds(pl.multiple_of(zone * 8, 8), 8)]
        return jnp.where(lax.rem(sub, 2) == 0, eight[:4], eight[4:])

    loads[4].wait()
    loads[5].wait()
    pick_build()
    loads[0].wait()
    loads[1].wait()
    for b in range(2):
        found = dot(pre[b], rhs[pl.ds(b * BLOCK, BLOCK)])
        for h in range(2):
            keep(0, h, b, found[:, h * 128 : h * 128 + 128])

    loads[2].wait()
    size_pre = largest_of(pre, 2)
    size_op = jnp.maximum(largest_of(diag, 2), OFF_MOST)
    pl.semaphore_wait(barrier, greeted)
    lane = lax.broadcasted_iota(jnp.int32, (1, 128), 1)
    size_start(0, jnp.where(lane < 64, size_pre, size_op))
    halo_start(0, 0)
    halo_start(0, 1)
    loads[6].wait()
    wells_start()
    contrib_start(0)
    loads[3].wait()
    loads[7].wait()
    loads[8].wait()
    local_products(0, 0)
    local_products(0, 1)
    size_start(1, size_finish(0))
    for h in range(2):
        halo_products(0, h)
        precondition(1, h, None)
        halo_start(1, h)

    contrib_start(1)
    local_products(1, 0)
    local_products(1, 1)
    lows_build()
    dense_start(0)
    scales = []

    def scale_of():
        if not scales:
            largest = size_finish(1)
            scales.append(1.0 / (largest[:, 0:1] * largest[:, 64:65]))
        return scales[0] * ALPHA

    for h in range(2):
        halo_products(1, h)
        precondition(2, h, scale_of)
        halo_start(2, h)

    shrink = scales[0]

    def makers(h, count):
        return [
            lambda rows: rhs[rows, pl.ds(h * 128, 128)].astype(F32) * ALPHA,
            lambda rows: image[0, h, rows] * ALPHA,
            lambda rows: image[1, h, rows] * (shrink * ALPHA),
            lambda rows: image[2, h, rows] * shrink,
        ][:count]

    contrib_start(2)
    early = [
        inner_products(makers(h, 3), [(0, 0), (0, 1), (0, 2), (1, 1), (1, 2), (2, 2)]) for h in range(2)
    ]
    red_start(0, 0, payload(early, 16))
    local_products(2, 0)
    local_products(2, 1)
    dense_start(1)
    late = []
    for h in range(2):
        halo_products(2, h)
        if h == 0:
            red_start(0, 1, red_finish(0, 0))
            dense_finish(0)
        late.append(inner_products(makers(h, 4), [(0, 3), (1, 3), (2, 3), (3, 3)]))
    red_start(1, 0, payload(late, 8))
    dense_start(2)
    red_start(1, 1, red_finish(1, 0))
    red_start(0, 2, red_finish(0, 1))
    dense_finish(1)
    owned = [own_wells(0)]
    red_start(1, 2, red_finish(1, 1))
    head = red_finish(0, 2)
    square, g0, g1, m00, m01, m11 = [head[2 * i : 2 * i + 2] for i in range(6)]
    dense_finish(2)
    owned.append(own_wells(1))
    tail = red_finish(1, 2)
    g2, m02, m12, m22 = [tail[2 * i : 2 * i + 2] for i in range(4)]

    norm = jnp.sqrt(square)
    g0, g1, g2 = [inner / norm for inner in (g0, g1, g2)]
    e01 = m01 / m00
    e02 = m02 / m00
    p11 = m11 - e01 * m01
    p12 = m12 - e01 * m02
    e12 = p12 / p11
    p22 = m22 - e02 * m02 - e12 * p12
    f0 = g0
    f1 = g1 - e01 * f0
    f2 = g2 - e02 * f0 - e12 * f1
    c2 = f2 / p22
    c1 = f1 / p11 - e12 * c2
    c0 = f0 / m00 - e01 * c1 - e02 * c2
    coeffs = [norm * c0, norm * (c1 * shrink), norm * (c2 * shrink) * (1.0 / ALPHA)]

    for part in range(4):
        rows = pl.ds(part * 192, 192)
        for h in range(2):
            total = coeffs[0][h : h + 1] * search[0, h, rows]
            for j in range(1, ITERS):
                total = total + coeffs[j][h : h + 1] * search[j, h, rows]
            adj_ref[rows, pl.ds(h * 128, 128)] = total

    owned.append(own_wells(2))
    gradient = jnp.zeros((4, R), F32)
    for j in range(ITERS):
        wide = jnp.concatenate([coeffs[j][0:1], coeffs[j][1:2]], axis=1)
        gradient = gradient + wide * owned[j]
    grad_ref[...] = gradient

    for j in range(ITERS):
        for h in range(2):
            for b in range(2):
                for kind in (SLOW, SIDE, FAST):
                    copy, sends, _ = halo(j, h, kind, b)
                    guarded(sends, copy.wait_send)
    for stage in range(2):
        rest = sizes[stage].at[pl.ds(0, sizes[stage].shape[0] - 1)]
        pltpu.make_async_copy(rest, rest, red_send.at[2, stage]).wait()
    for which in range(2):
        for stage in range(3):
            seven = reds[which].at[stage, pl.ds(0, 7)]
            pltpu.make_async_copy(seven, seven, red_send.at[which, stage]).wait()
    for j in range(ITERS):
        fifteen = spread.at[j, pl.ds(0, 15)]
        pltpu.make_async_copy(fifteen, fifteen, well_send.at[j]).wait()
        most = partial.at[j, pl.ds(0, 31)]
        pltpu.make_async_copy(most, most, well_send.at[4 + j]).wait()
        most = final.at[j, pl.ds(0, 31)]
        pltpu.make_async_copy(most, most, well_send.at[7 + j]).wait()
    fifteen = wells.at[pl.ds(0, 15)]
    pltpu.make_async_copy(fifteen, fifteen, well_send.at[3]).wait()


def shards(
    diag_blocks,
    precond_blocks,
    offdiag_blocks,
    offdiag_col,
    slot_live,
    adjoint_rhs,
    perf_cell,
    perf_well,
    perf_coeff,
):
    any_spec = pl.BlockSpec(memory_space=pl.ANY)
    vmem = pl.BlockSpec(memory_space=pltpu.VMEM)
    dma = pltpu.SemaphoreType.DMA
    adjoint, gradient = pl.pallas_call(
        kernel,
        out_shape=(
            pltpu.VMEM((ROWS, R), F32),
            pltpu.VMEM((4, R), F32),
        ),
        in_specs=[any_spec] * 9,
        out_specs=(vmem, vmem),
        scratch_shapes=[
            pltpu.SMEM((2, 4), jnp.int32),
            pltpu.SMEM((2, 4), jnp.int32),
            pltpu.VMEM((1, 128), jnp.int32),
            pltpu.VMEM((1, 128), jnp.int32),
            pltpu.VMEM((3, 1, 128), F32),
            pltpu.VMEM((2, BLOCK, BLOCK), BF),
            pltpu.VMEM((2, BLOCK, BLOCK), BF),
            pltpu.VMEM((8, BLOCK, BLOCK), BF),
            pltpu.VMEM((ROWS, R), BF),
            pltpu.VMEM((ITERS, 2, ROWS, 128), F32),
            pltpu.VMEM((ITERS, 2, ROWS, 128), F32),
            pltpu.VMEM((ITERS, 2, ROWS, 128), BF),
            pltpu.VMEM((ITERS, 2, ROWS, 128), BF),
            pltpu.VMEM((ITERS, 2, 2, BLOCK, 128), BF),
            pltpu.VMEM((ITERS, 2, 2, BLOCK, 128), BF),
            pltpu.VMEM((ITERS, 2, 2, BLOCK, 128), BF),
            pltpu.VMEM((16, 1, 128), F32),
            pltpu.VMEM((32, 1, 128), F32),
            pltpu.VMEM((3, 8, 16, 128), F32),
            pltpu.VMEM((3, 8, 8, 128), F32),
            pltpu.VMEM((256, ROWS), BF),
            pltpu.VMEM((16, 1, 128), jnp.int32),
            pltpu.VMEM((128, 2048), BF),
            pltpu.VMEM((16, 256, 128), BF),
            pltpu.VMEM((ITERS, 16, 16, 128), F32),
            pltpu.VMEM((ITERS, 16, 16, 128), F32),
            pltpu.VMEM((512, 2048), BF),
            pltpu.VMEM((ITERS, 32, 8, 128), F32),
            pltpu.VMEM((ITERS, 32, 8, 128), F32),
            pltpu.VMEM((ITERS, 32, 8, 128), F32),
            pltpu.VMEM((128, R), F32),
            dma((9,)),
            dma((ITERS, 2, 6)),
            dma((ITERS, 2, 6)),
            dma((3, 3)),
            dma((3, 3)),
            dma((10,)),
            dma((10,)),
        ],
        compiler_params=pltpu.CompilerParams(
            collective_id=0, has_side_effects=True, vmem_limit_bytes=60 * 1024 * 1024
        ),
        name="adjoint_solve",
    )(
        diag_blocks.reshape(2, BLOCK, BLOCK),
        precond_blocks.reshape(2, BLOCK, BLOCK),
        offdiag_blocks.reshape(8, BLOCK, BLOCK),
        adjoint_rhs.reshape(ROWS, R),
        offdiag_col.reshape(2, 4),
        slot_live.reshape(2, 4),
        perf_cell.reshape(1, 128),
        perf_well.reshape(1, 128),
        perf_coeff.reshape(3, 1, 128),
    )
    return adjoint.reshape(1, 1, 2, BLOCK, R), gradient


def solution(mesh):
    placed = (
        P("zone", "sub", None, None, None),
        P("zone", "sub", None, None, None),
        P("zone", "sub", None, None, None, None),
        P("zone", "sub", None, None),
        P("zone", "sub", None, None),
        P("zone", "sub", None, None, None),
        P("zone", "sub", None),
        P("zone", "sub", None),
        P("zone", "sub", None, None),
    )
    return jax.shard_map(
        shards,
        mesh=mesh,
        in_specs=placed,
        out_specs=(P("zone", "sub", None, None, None), P(("zone", "sub"), None)),
        check_vma=False,
    )
```

```python
import functools

import jax
import jax.numpy as jnp
from jax import lax
from jax.experimental import pallas as pl
from jax.experimental.pallas import tpu as pltpu
from jax.sharding import PartitionSpec as P

MESH = pl.DeviceIdType.MESH
BF = jnp.bfloat16
F32 = jnp.float32
BLOCK = 384
ROWS = 768
R = 256
ITERS = 3
OFF_MOST = 0.09375
ALPHA = 2.0**-12
FAST, SLOW, SIDE = 0, 2, 4


def place():
    zone = lax.axis_index("zone")
    sub = lax.axis_index("sub")
    return zone, sub, zone // 2, lax.rem(zone, 2), sub // 4, lax.rem(sub, 4)


def layout():
    _, _, y, core, z, x = place()
    twice = [2 * lax.rem(y + step, 8) for step in range(8)]
    cores = [core, 1 - core]
    layers = [lax.rem(z + step, 8) for step in range(8)]
    across = [lax.rem(x + step, 4) for step in range(4)]
    pair = [lax.rem(x, 2), 1 - lax.rem(x, 2)]
    aside = x - pair[0]
    one, two, four, eight = [(0,), (0, 1), range(4), range(8)]
    spans = {
        "xc": (one, two, one, four, lambda q, c, l, a: c * 4 + a),
        "y": (eight, one, one, one, lambda q, c, l, a: q // 2),
        "z": (one, one, eight, one, lambda q, c, l, a: l),
        "zone": (eight, two, one, one, lambda q, c, l, a: q + c),
        "sub": (one, one, eight, four, lambda q, c, l, a: l * 4 + a),
        "pair": (eight, two, one, two, lambda q, c, l, a: (q + c) * 2 + a),
    }
    groups = {}
    for name, (dys, dcs, dzs, dxs, slot_of) in spans.items():
        found = []
        for dy in dys:
            for dc in dcs:
                for dz in dzs:
                    for dx in dxs:
                        hops = min(dy, 8 - dy) + min(dz, 8 - dz) + min(dx, 4 - dx) + 0.4 * dc
                        a = pair[dx] if name == "pair" else across[dx]
                        slot = slot_of(twice[dy], cores[dc], layers[dz], a)
                        where = aside + a if name == "pair" else a
                        device = (twice[dy] + cores[dc], layers[dz] * 4 + where)
                        found.append((hops, slot, device))
        groups[name] = (found[0][1], [(slot, device) for hops, slot, device in sorted(found[1:], key=lambda e: -e[0])])
    return groups


def split(value):
    high = value.astype(BF)
    return high, (value - high.astype(F32)).astype(BF)


def dot(left, right):
    return jnp.dot(left, right, preferred_element_type=F32)


def kernel(
    diag_hbm,
    pre_hbm,
    off_hbm,
    rhs_hbm,
    col_hbm,
    live_hbm,
    cell_hbm,
    well_hbm,
    coeff_hbm,
    adj_ref,
    grad_ref,
    col_ref,
    live_ref,
    cell_ref,
    well_ref,
    coeff_ref,
    diag,
    pre,
    off,
    rhs,
    search,
    image,
    high,
    low,
    near,
    far,
    side,
    size0,
    size1,
    red1,
    red2,
    pick,
    wells,
    lows,
    hots,
    contrib,
    spread,
    placed,
    dense,
    partial,
    final,
    turned,
    load_sem,
    halo_send,
    halo_recv,
    red_send,
    red_recv,
    well_send,
    well_recv,
):
    zone, sub, y, core, z, x = place()
    sizes = (size0, size1)
    reds = (red1, red2)
    groups = layout()

    def others(name):
        return groups[name][1]

    loads = [
        pltpu.make_async_copy(src, dst, load_sem.at[i])
        for i, (src, dst) in enumerate(
            (
                (pre_hbm, pre),
                (rhs_hbm, rhs),
                (diag_hbm, diag),
                (off_hbm, off),
                (cell_hbm, cell_ref),
                (coeff_hbm, coeff_ref),
                (well_hbm, well_ref),
                (col_hbm, col_ref),
                (live_hbm, live_ref),
            )
        )
    ]
    for load in loads:
        load.start()

    barrier = pltpu.get_barrier_semaphore()
    greeted = 0
    for name in ("zone", "sub", "pair", "xc"):
        for _, device in others(name):
            pl.semaphore_signal(barrier, inc=1, device_id=device, device_id_type=MESH)
            greeted += 1

    mate = (zone + 1 - 2 * core, sub)
    beyond = (zone - 1 + 2 * core, sub)
    has_far = jnp.logical_and(beyond[0] >= 0, beyond[0] < 16)
    has_side = (sub > 0, sub < 31)
    side_dev = ((zone, sub - 1), (zone, sub + 1))

    @pl.when(jnp.logical_not(has_far))
    def _():
        far[...] = jnp.zeros(far.shape, BF)

    for b in range(2):

        @pl.when(jnp.logical_not(has_side[b]))
        def _():
            side[:, :, b] = jnp.zeros((ITERS, 2, BLOCK, 128), BF)

    def halo(j, h, kind, b):
        src = high.at[j, h, pl.ds(b * BLOCK, BLOCK)]
        dst, device, sends, receives = {
            SIDE: (side.at[j, h, 1 - b], side_dev[b], has_side[b], has_side[1 - b]),
            SLOW: (far.at[j, h, b], beyond, has_far, has_far),
            FAST: (near.at[j, h, b], mate, None, None),
        }[kind]
        copy = pltpu.make_async_remote_copy(
            src,
            dst,
            halo_send.at[j, h, kind + b],
            halo_recv.at[j, h, kind + b],
            device_id=device,
            device_id_type=MESH,
        )
        return copy, sends, receives

    def guarded(condition, action):
        if condition is None:
            action()
        else:
            pl.when(condition)(action)

    def halo_start(j, h):
        for b in range(2):
            for kind in (SLOW, SIDE, FAST):
                copy, sends, _ = halo(j, h, kind, b)
                guarded(sends, copy.start)

    def halo_wait(j, h, kind):
        for b in range(2):
            copy, _, receives = halo(j, h, kind, b)
            guarded(receives, copy.wait_recv)

    def keep(j, h, b, found):
        rows = pl.ds(b * BLOCK, BLOCK)
        search[j, h, rows] = found
        upper, lower = split(found)
        high[j, h, rows] = upper
        low[j, h, rows] = lower

    def both(left, upper, lower):
        found = dot(left, jnp.concatenate([upper, lower], axis=1))
        return found[:, :128] + found[:, 128:]

    def precondition(j, h, scale):
        for b in range(2):
            upper, lower = split(image[j - 1, h, pl.ds(b * BLOCK, BLOCK)])
            found = both(pre[b], upper, lower)
            keep(j, h, b, found if scale is None else found * scale())

    def slot_of(b, position):
        where = 0
        for k in range(1, 4):
            where = where + jnp.where(col_ref[b, k] == position, k, 0)
        return b * 4 + where

    def live_of(b, position):
        found = 0
        for k in range(4):
            found = found + jnp.where(col_ref[b, k] == position, live_ref[b, k], 0)
        return found

    def local_products(j, h):
        for b in range(2):
            mine = pl.ds(b * BLOCK, BLOCK)
            other = pl.ds((1 - b) * BLOCK, BLOCK)
            total = both(diag[b], high[j, h, mine], low[j, h, mine])
            inner = both(off[slot_of(b, 6 - b)], high[j, h, other], low[j, h, other])
            image[j, h, mine] = total + jnp.where(live_of(b, 6 - b) > 0, inner, 0.0)

    def halo_products(j, h):
        def add(b, position, block):
            image[j, h, pl.ds(b * BLOCK, BLOCK)] += dot(off[slot_of(b, position)], block)

        halo_wait(j, h, FAST)
        for b in range(2):
            add(b, jnp.where(core == 0, 9 + b, 1 + b), near[j, h, b])
        halo_wait(j, h, SIDE)
        for b in range(2):
            add(b, 4 + 3 * b, side[j, h, b])
        halo_wait(j, h, SLOW)
        for b in range(2):
            add(b, jnp.where(core == 0, 1 + b, 9 + b), far[j, h, b])

    stages = ("xc", "y", "z")

    def red_start(which, stage, value):
        buf = reds[which].at[stage]
        me = groups[stages[stage]][0]
        buf[me] = value
        for _, device in others(stages[stage]):
            pltpu.make_async_remote_copy(
                buf.at[me],
                buf.at[me],
                red_send.at[which, stage],
                red_recv.at[which, stage],
                device_id=device,
                device_id_type=MESH,
            ).start()

    def red_finish(which, stage):
        buf = reds[which].at[stage]
        seven = buf.at[pl.ds(0, 7)]
        pltpu.make_async_copy(seven, seven, red_recv.at[which, stage]).wait()
        total = buf[0]
        for i in range(1, 8):
            total = total + buf[i]
        return total

    def size_start(stage, value):
        name = ("zone", "sub")[stage]
        buf = sizes[stage]
        me = groups[name][0]
        buf[me] = value
        for _, device in others(name):
            pltpu.make_async_remote_copy(
                buf.at[me],
                buf.at[me],
                red_send.at[2, stage],
                red_recv.at[2, stage],
                device_id=device,
                device_id_type=MESH,
            ).start()

    def size_finish(stage):
        buf = sizes[stage]
        count = buf.shape[0]
        rest = buf.at[pl.ds(0, count - 1)]
        pltpu.make_async_copy(rest, rest, red_recv.at[2, stage]).wait()
        total = buf[0]
        for i in range(1, count):
            total = jnp.maximum(total, buf[i])
        return total

    def inner_products(makers, pairs):
        step = 128

        def body(i, sums):
            rows = pl.ds(pl.multiple_of(i * step, step), step)
            vectors = [make(rows) for make in makers]
            return tuple(
                total + jnp.sum((vectors[a] * vectors[c]).reshape(step // 8, 8, 128), axis=0)
                for total, (a, c) in zip(sums, pairs)
            )

        sums = lax.fori_loop(
            0, ROWS // step, body, tuple(jnp.zeros((8, 128), F32) for _ in pairs)
        )
        return [jnp.sum(total, axis=0, keepdims=True) for total in sums]

    def payload(values, rows):
        pieces = [half for pair in zip(*values) for half in pair]
        if len(pieces) < rows:
            pieces.append(jnp.zeros((rows - len(pieces), 128), F32))
        return jnp.concatenate(pieces, axis=0)

    def largest_of(ref, count):
        def body(i, best):
            return jnp.maximum(best, jnp.max(jnp.abs(ref[i].astype(F32).reshape(48, 8, BLOCK)), axis=0))

        best = lax.fori_loop(0, count, body, jnp.zeros((8, BLOCK), F32))
        return jnp.max(jnp.max(best, axis=0, keepdims=True), axis=1, keepdims=True)

    def wells_start():
        wells[zone] = well_ref[...]
        for _, device in others("zone"):
            pltpu.make_async_remote_copy(
                wells.at[zone],
                wells.at[zone],
                well_send.at[3],
                well_recv.at[3],
                device_id=device,
                device_id_type=MESH,
            ).start()

    def pick_build():
        cells = cell_ref[...]
        for b in range(2):
            for q in range(3):
                row = lax.broadcasted_iota(jnp.int32, (128, 128), 0) + b * 128
                upper, lower = split(jnp.where(row == cells, -coeff_ref[q], 0.0).T)
                columns = pl.ds(b * BLOCK + q * 128, 128)
                pick[pl.ds(0, 128), columns] = upper
                pick[pl.ds(128, 128), columns] = lower

    def lows_build():
        fifteen = wells.at[pl.ds(0, 15)]
        pltpu.make_async_copy(fifteen, fifteen, well_recv.at[3]).wait()

        def body(i, carry):
            ids = wells[i]
            code = ((ids >> 7) << 3) + (ids & 7)
            row = lax.broadcasted_iota(jnp.int32, (128, 128), 0)
            columns = pl.ds(pl.multiple_of(i * 128, 128), 128)
            lows[:, columns] = jnp.where(row == code, 1.0, 0.0).astype(BF)
            chunk = jnp.broadcast_to((ids >> 3) & 15, (16, 128))
            for k in range(16):
                hots[i, pl.ds(k * 16, 16)] = jnp.where(chunk == k, 1.0, 0.0).astype(BF)
            return carry

        lax.fori_loop(0, 16, body, 0)

    def contrib_start(j):
        upper = jnp.concatenate([high[j, 0], high[j, 1]], axis=1)
        lower = jnp.concatenate([low[j, 0], low[j, 1]], axis=1)
        value = dot(pick[...], upper)
        value = value[:128] + value[128:] + dot(pick[pl.ds(0, 128)], lower)
        contrib[j] = jnp.concatenate([value[:, :128].T, value[:, 128:].T], axis=0).reshape(16, 16, 128)
        spread[j, zone] = contrib[j, zone]
        for slot, device in others("zone"):
            pltpu.make_async_remote_copy(
                contrib.at[j, slot],
                spread.at[j, zone],
                well_send.at[j],
                well_recv.at[j],
                device_id=device,
                device_id_type=MESH,
            ).start()

    def dense_start(j):
        fifteen = spread.at[j, pl.ds(0, 15)]
        pltpu.make_async_copy(fifteen, fifteen, well_recv.at[j]).wait()

        def body(i, carry):
            upper, lower = split(spread[j, i])
            columns = pl.ds(pl.multiple_of(i * 128, 128), 128)
            hot = hots[i]
            placed[pl.ds(0, 256), columns] = jnp.concatenate([upper] * 16, axis=0) * hot
            placed[pl.ds(256, 256), columns] = jnp.concatenate([lower] * 16, axis=0) * hot
            return carry

        lax.fori_loop(0, 16, body, 0)
        total = lax.dot_general(
            placed[...], lows[...], (((1,), (1,)), ((), ())), preferred_element_type=F32
        )
        dense[j] = (total[:256] + total[256:]).reshape(32, 8, 128)
        partial[j, sub] = dense[j, sub]
        for slot, device in others("sub"):
            pltpu.make_async_remote_copy(
                dense.at[j, slot],
                partial.at[j, sub],
                well_send.at[4 + j],
                well_recv.at[4 + j],
                device_id=device,
                device_id_type=MESH,
            ).start()

    def dense_finish(j):
        most = partial.at[j, pl.ds(0, 31)]
        pltpu.make_async_copy(most, most, well_recv.at[4 + j]).wait()
        total = partial[j, 0]
        for i in range(1, 32):
            total = total + partial[j, i]
        me = groups["pair"][0]
        final[j, me] = total
        for _, device in others("pair"):
            pltpu.make_async_remote_copy(
                final.at[j, me],
                final.at[j, me],
                well_send.at[7 + j],
                well_recv.at[7 + j],
                device_id=device,
                device_id_type=MESH,
            ).start()

    def own_wells(j):
        most = final.at[j, pl.ds(0, 31)]
        pltpu.make_async_copy(most, most, well_recv.at[7 + j]).wait()
        gathered = final[j].reshape(R, 128)
        turned[...] = jnp.concatenate([gathered[:128].T, gathered[128:].T], axis=1)
        eight = turned[pl.ds(pl.multiple_of(zone * 8, 8), 8)]
        return jnp.where(lax.rem(sub, 2) == 0, eight[:4], eight[4:])

    loads[4].wait()
    loads[5].wait()
    pick_build()
    loads[0].wait()
    loads[1].wait()
    for b in range(2):
        found = dot(pre[b], rhs[pl.ds(b * BLOCK, BLOCK)])
        for h in range(2):
            keep(0, h, b, found[:, h * 128 : h * 128 + 128])

    loads[2].wait()
    size_pre = largest_of(pre, 2)
    size_op = jnp.maximum(largest_of(diag, 2), OFF_MOST)
    pl.semaphore_wait(barrier, greeted)
    lane = lax.broadcasted_iota(jnp.int32, (1, 128), 1)
    size_start(0, jnp.where(lane < 64, size_pre, size_op))
    halo_start(0, 0)
    halo_start(0, 1)
    loads[6].wait()
    wells_start()
    contrib_start(0)
    loads[3].wait()
    loads[7].wait()
    loads[8].wait()
    local_products(0, 0)
    size_start(1, size_finish(0))
    local_products(0, 1)
    for h in range(2):
        halo_products(0, h)
        precondition(1, h, None)
        halo_start(1, h)

    contrib_start(1)
    local_products(1, 0)
    local_products(1, 1)
    lows_build()
    dense_start(0)
    scales = []

    def scale_of():
        if not scales:
            largest = size_finish(1)
            scales.append(1.0 / (largest[:, 0:1] * largest[:, 64:65]))
        return scales[0] * ALPHA

    for h in range(2):
        halo_products(1, h)
        precondition(2, h, scale_of)
        halo_start(2, h)

    shrink = scales[0]

    def makers(h, count):
        return [
            lambda rows: rhs[rows, pl.ds(h * 128, 128)].astype(F32) * ALPHA,
            lambda rows: image[0, h, rows] * ALPHA,
            lambda rows: image[1, h, rows] * (shrink * ALPHA),
            lambda rows: image[2, h, rows] * shrink,
        ][:count]

    contrib_start(2)
    early = [
        inner_products(makers(h, 3), [(0, 0), (0, 1), (0, 2), (1, 1), (1, 2), (2, 2)]) for h in range(2)
    ]
    red_start(0, 0, payload(early, 16))
    local_products(2, 0)
    local_products(2, 1)
    dense_start(1)
    late = []
    for h in range(2):
        halo_products(2, h)
        if h == 0:
            red_start(0, 1, red_finish(0, 0))
            dense_finish(0)
        late.append(inner_products(makers(h, 4), [(0, 3), (1, 3), (2, 3), (3, 3)]))
    red_start(1, 0, payload(late, 8))
    dense_start(2)
    red_start(1, 1, red_finish(1, 0))
    red_start(0, 2, red_finish(0, 1))
    dense_finish(1)
    red_start(1, 2, red_finish(1, 1))
    owned = [own_wells(0)]
    head = red_finish(0, 2)
    square, g0, g1, m00, m01, m11 = [head[2 * i : 2 * i + 2] for i in range(6)]
    dense_finish(2)
    owned.append(own_wells(1))
    tail = red_finish(1, 2)
    g2, m02, m12, m22 = [tail[2 * i : 2 * i + 2] for i in range(4)]

    norm = jnp.sqrt(square)
    g0, g1, g2 = [inner / norm for inner in (g0, g1, g2)]
    e01 = m01 / m00
    e02 = m02 / m00
    p11 = m11 - e01 * m01
    p12 = m12 - e01 * m02
    e12 = p12 / p11
    p22 = m22 - e02 * m02 - e12 * p12
    f0 = g0
    f1 = g1 - e01 * f0
    f2 = g2 - e02 * f0 - e12 * f1
    c2 = f2 / p22
    c1 = f1 / p11 - e12 * c2
    c0 = f0 / m00 - e01 * c1 - e02 * c2
    coeffs = [norm * c0, norm * (c1 * shrink), norm * (c2 * shrink) * (1.0 / ALPHA)]

    for part in range(4):
        rows = pl.ds(part * 192, 192)
        for h in range(2):
            total = coeffs[0][h : h + 1] * search[0, h, rows]
            for j in range(1, ITERS):
                total = total + coeffs[j][h : h + 1] * search[j, h, rows]
            adj_ref[rows, pl.ds(h * 128, 128)] = total

    owned.append(own_wells(2))
    gradient = jnp.zeros((4, R), F32)
    for j in range(ITERS):
        wide = jnp.concatenate([coeffs[j][0:1], coeffs[j][1:2]], axis=1)
        gradient = gradient + wide * owned[j]
    grad_ref[...] = gradient

    for j in range(ITERS):
        for h in range(2):
            for b in range(2):
                for kind in (SLOW, SIDE, FAST):
                    copy, sends, _ = halo(j, h, kind, b)
                    guarded(sends, copy.wait_send)
    for stage in range(2):
        rest = sizes[stage].at[pl.ds(0, sizes[stage].shape[0] - 1)]
        pltpu.make_async_copy(rest, rest, red_send.at[2, stage]).wait()
    for which in range(2):
        for stage in range(3):
            seven = reds[which].at[stage, pl.ds(0, 7)]
            pltpu.make_async_copy(seven, seven, red_send.at[which, stage]).wait()
    for j in range(ITERS):
        fifteen = spread.at[j, pl.ds(0, 15)]
        pltpu.make_async_copy(fifteen, fifteen, well_send.at[j]).wait()
        most = partial.at[j, pl.ds(0, 31)]
        pltpu.make_async_copy(most, most, well_send.at[4 + j]).wait()
        most = final.at[j, pl.ds(0, 31)]
        pltpu.make_async_copy(most, most, well_send.at[7 + j]).wait()
    fifteen = wells.at[pl.ds(0, 15)]
    pltpu.make_async_copy(fifteen, fifteen, well_send.at[3]).wait()


def shards(
    diag_blocks,
    precond_blocks,
    offdiag_blocks,
    offdiag_col,
    slot_live,
    adjoint_rhs,
    perf_cell,
    perf_well,
    perf_coeff,
):
    any_spec = pl.BlockSpec(memory_space=pl.ANY)
    vmem = pl.BlockSpec(memory_space=pltpu.VMEM)
    dma = pltpu.SemaphoreType.DMA
    adjoint, gradient = pl.pallas_call(
        kernel,
        out_shape=(
            pltpu.VMEM((ROWS, R), F32),
            pltpu.VMEM((4, R), F32),
        ),
        in_specs=[any_spec] * 9,
        out_specs=(vmem, vmem),
        scratch_shapes=[
            pltpu.SMEM((2, 4), jnp.int32),
            pltpu.SMEM((2, 4), jnp.int32),
            pltpu.VMEM((1, 128), jnp.int32),
            pltpu.VMEM((1, 128), jnp.int32),
            pltpu.VMEM((3, 1, 128), F32),
            pltpu.VMEM((2, BLOCK, BLOCK), BF),
            pltpu.VMEM((2, BLOCK, BLOCK), BF),
            pltpu.VMEM((8, BLOCK, BLOCK), BF),
            pltpu.VMEM((ROWS, R), BF),
            pltpu.VMEM((ITERS, 2, ROWS, 128), F32),
            pltpu.VMEM((ITERS, 2, ROWS, 128), F32),
            pltpu.VMEM((ITERS, 2, ROWS, 128), BF),
            pltpu.VMEM((ITERS, 2, ROWS, 128), BF),
            pltpu.VMEM((ITERS, 2, 2, BLOCK, 128), BF),
            pltpu.VMEM((ITERS, 2, 2, BLOCK, 128), BF),
            pltpu.VMEM((ITERS, 2, 2, BLOCK, 128), BF),
            pltpu.VMEM((16, 1, 128), F32),
            pltpu.VMEM((32, 1, 128), F32),
            pltpu.VMEM((3, 8, 16, 128), F32),
            pltpu.VMEM((3, 8, 8, 128), F32),
            pltpu.VMEM((256, ROWS), BF),
            pltpu.VMEM((16, 1, 128), jnp.int32),
            pltpu.VMEM((128, 2048), BF),
            pltpu.VMEM((16, 256, 128), BF),
            pltpu.VMEM((ITERS, 16, 16, 128), F32),
            pltpu.VMEM((ITERS, 16, 16, 128), F32),
            pltpu.VMEM((512, 2048), BF),
            pltpu.VMEM((ITERS, 32, 8, 128), F32),
            pltpu.VMEM((ITERS, 32, 8, 128), F32),
            pltpu.VMEM((ITERS, 32, 8, 128), F32),
            pltpu.VMEM((128, R), F32),
            dma((9,)),
            dma((ITERS, 2, 6)),
            dma((ITERS, 2, 6)),
            dma((3, 3)),
            dma((3, 3)),
            dma((10,)),
            dma((10,)),
        ],
        compiler_params=pltpu.CompilerParams(
            collective_id=0, has_side_effects=True, vmem_limit_bytes=60 * 1024 * 1024
        ),
        name="adjoint_solve",
    )(
        diag_blocks.reshape(2, BLOCK, BLOCK),
        precond_blocks.reshape(2, BLOCK, BLOCK),
        offdiag_blocks.reshape(8, BLOCK, BLOCK),
        adjoint_rhs.reshape(ROWS, R),
        offdiag_col.reshape(2, 4),
        slot_live.reshape(2, 4),
        perf_cell.reshape(1, 128),
        perf_well.reshape(1, 128),
        perf_coeff.reshape(3, 1, 128),
    )
    return adjoint.reshape(1, 1, 2, BLOCK, R), gradient


def solution(mesh):
    placed = (
        P("zone", "sub", None, None, None),
        P("zone", "sub", None, None, None),
        P("zone", "sub", None, None, None, None),
        P("zone", "sub", None, None),
        P("zone", "sub", None, None),
        P("zone", "sub", None, None, None),
        P("zone", "sub", None),
        P("zone", "sub", None),
        P("zone", "sub", None, None),
    )
    return jax.shard_map(
        shards,
        mesh=mesh,
        in_specs=placed,
        out_specs=(P("zone", "sub", None, None, None), P(("zone", "sub"), None)),
        check_vma=False,
    )
```
